32 devices in a mesh: wide: 16 (over z, x, core), tensor: 2 (over y).
Axes of the slice: x: 2, y: 2, z: 4, core: 2. Of those that a mesh axis runs over, the one named last changes fastest.
Arguments:
- tokens: bfloat16 [4, 2, 1024, 1152], P(None, None, ('wide', 'tensor')), may hold values from -6 to 6
- out_grad: bfloat16 [4, 2, 1024, 1152], P(None, None, ('wide', 'tensor')), may hold values from -6 to 6
- doc_lengths: int32 [4, 2, 3], replicated, may hold values from 0 to 1024, as said below
- picture_starts: int32 [4, 2, 4], replicated, may hold values from 0 to 768, as said below
- q_weight: bfloat16 [1152, 1024], P('wide', 'tensor'), may hold values from -0.1875 to 0.1875
- k_weight: bfloat16 [1152, 256], P('wide'), may hold values from -0.1875 to 0.1875
- v_weight: bfloat16 [1152, 256], P('wide'), may hold values from -0.1875 to 0.1875
- out_weight: bfloat16 [1152, 1024], P('wide', 'tensor'), may hold values from -0.1875 to 0.1875
- gate_weight: bfloat16 [1152, 6912], P('wide', 'tensor'), may hold values from -0.1875 to 0.1875
- up_weight: bfloat16 [1152, 6912], P('wide', 'tensor'), may hold values from -0.1875 to 0.1875
- down_weight: bfloat16 [1152, 6912], P('wide', 'tensor'), may hold values from -0.078125 to 0.078125
- attn_in_gain: bfloat16 [1152], P('wide'), may hold values from 0.5 to 1.5
- attn_out_gain: bfloat16 [1152], P('wide'), may hold values from 0.5 to 1.5
- ffn_in_gain: bfloat16 [1152], P('wide'), may hold values from 0.5 to 1.5
- ffn_out_gain: bfloat16 [1152], P('wide'), may hold values from 0.5 to 1.5
- query_gain: bfloat16 [256], P('wide'), may hold values from 0.25 to 1.75
- key_gain: bfloat16 [256], P('wide'), may hold values from 0.25 to 1.75
Outputs:
- output: bfloat16 [4, 2, 1024, 1152], P(None, None, ('wide', 'tensor'))
- input_grad: bfloat16 [4, 2, 1024, 1152], P(None, None, ('wide', 'tensor'))
- q_weight_grad: float32 [1152, 1024], P('wide', 'tensor')
- k_weight_grad: float32 [1152, 256], P('wide')
- v_weight_grad: float32 [1152, 256], P('wide')
- out_weight_grad: float32 [1152, 1024], P('wide', 'tensor')
- gate_weight_grad: float32 [1152, 6912], P('wide', 'tensor')
- up_weight_grad: float32 [1152, 6912], P('wide', 'tensor')
- down_weight_grad: float32 [1152, 6912], P('wide', 'tensor')
- attn_in_gain_grad: float32 [1152], P('wide')
- attn_out_gain_grad: float32 [1152], P('wide')
- ffn_in_gain_grad: float32 [1152], P('wide')
- ffn_out_gain_grad: float32 [1152], P('wide')
- query_gain_grad: float32 [256], P('wide')
- key_gain_grad: float32 [256], P('wide')
The draws below stay inside these ranges and needn't reach their ends.
Inputs may be any that keep to these rules, and one draw needn't show every extreme that they name: `doc_lengths`: each row sums to 1024; a zero is an empty document; in one sequence, chosen by the seed, the whole sequence is one document. `picture_starts`: picture block i starts within positions i * 256 to (i + 1) * 256 - 256, so blocks never intersect.
All inputs are finite; a program needn't handle non-finite values.
Results may differ from the reference program's by a relative error of at most 0.02.
Values may be sent and summed in bfloat16 or wider, within the bound.
No kernel may reach another device: no remote copies, remote signals or barrier semaphores. Data moves between devices by JAX's collectives and lax.ppermute only.
A program may use at most 256 MiB of HBM per device.

```python
import math
import jax
import jax.numpy as jnp
from jax import lax

D = 1152
HEADS = 4
HD = 256
FF = 6912
MICRO = 4
SEQS = 2
DOCS = 3
PICS = 4
PIC = 256
LENGTH = 1024


def draw_doc_lengths(key, part):
    key = jax.random.fold_in(key, 11)
    whole_key, cut_key = jax.random.split(key)
    total_seqs = MICRO * SEQS
    single = jax.random.randint(whole_key, (), 0, total_seqs)
    cut_points = jnp.sort(jax.random.randint(cut_key, (total_seqs, DOCS - 1), 0, LENGTH + 1), axis=1)
    boundaries = jnp.concatenate([jnp.zeros((total_seqs, 1), jnp.int32), cut_points.astype(jnp.int32), jnp.full((total_seqs, 1), LENGTH, jnp.int32)], axis=1)
    lengths = boundaries[:, 1:] - boundaries[:, :-1]
    slot_ids = jnp.arange(DOCS, dtype=jnp.int32)
    lonely = jnp.where(slot_ids == 0, LENGTH, 0).astype(jnp.int32)
    chosen_row = jnp.arange(total_seqs, dtype=jnp.int32)[:, None] == single
    result = jnp.where(chosen_row, lonely[None, :], lengths).astype(jnp.int32)
    return result.reshape(MICRO, SEQS, DOCS)


def draw_picture_starts(key, part):
    key = jax.random.fold_in(key, 23)
    pick_key, shift_key = jax.random.split(key)
    total_seqs = MICRO * SEQS
    region = LENGTH // PICS
    flush = jax.random.randint(pick_key, (), 0, total_seqs)
    offsets = jax.random.randint(shift_key, (total_seqs, PICS), 0, region - PIC + 1)
    slot_ids = jnp.arange(PICS, dtype=jnp.int32)[None, :]
    chosen_row = jnp.arange(total_seqs, dtype=jnp.int32)[:, None] == flush
    offsets = jnp.where(chosen_row & (slot_ids == 0), 0, offsets)
    offsets = jnp.where(chosen_row & (slot_ids == PICS - 1), region - PIC, offsets)
    return (slot_ids * region + offsets).astype(jnp.int32).reshape(MICRO, SEQS, PICS)


def level_of(own_key, extent, shards, least, largest):
    level = 1.0
    for dim, blocks in shards:
        draws = jax.random.uniform(jax.random.fold_in(jax.random.fold_in(own_key, 6), dim), (blocks,), jnp.float32, least / len(shards), largest / len(shards))
        level = level * jnp.repeat(jnp.exp(draws), extent[dim] // blocks).reshape((-1,) + (1,) * (len(extent) - 1 - dim))
    return level


def centred(own_key, shape, spread, reach, pieces=(), kind=jnp.bfloat16):
    loudness = level_of(own_key, shape, pieces, -0.22, 0.18) if pieces else 1.0
    array = jax.random.normal(own_key, shape, jnp.float32) * spread * loudness
    return jnp.minimum(jnp.maximum(array, -reach), reach).astype(kind)


def setup_inputs(seed: int = 0) -> dict:
    keys = jax.random.split(jax.random.key(seed), 18)
    tokens = centred(keys[0], (MICRO, SEQS, LENGTH, D), 1.0, 6.0, ((2, 32),))
    out_grad = centred(keys[1], (MICRO, SEQS, LENGTH, D), 1.0, 6.0, ((2, 32),))
    doc_lengths = draw_doc_lengths(jax.random.fold_in(keys[17], 71), 0)
    picture_starts = draw_picture_starts(jax.random.fold_in(keys[17], 71), 0)
    q_weight = centred(keys[4], (D, HEADS * HD), D ** -0.5, 0.1875, ((0, 16), (1, 2)))
    k_weight = centred(keys[5], (D, HD), D ** -0.5, 0.1875, ((0, 16),))
    v_weight = centred(keys[6], (D, HD), D ** -0.5, 0.1875, ((0, 16),))
    out_weight = centred(keys[7], (D, HEADS * HD), (HEADS * HD) ** -0.5, 0.1875, ((0, 16), (1, 2)))
    gate_weight = centred(keys[8], (D, FF), D ** -0.5, 0.1875, ((0, 16), (1, 2)))
    up_weight = centred(keys[9], (D, FF), D ** -0.5, 0.1875, ((0, 16), (1, 2)))
    down_weight = centred(keys[10], (D, FF), FF ** -0.5, 0.078125, ((0, 16), (1, 2)))
    attn_in_gain = jnp.clip(1.0 + 0.1 * jax.random.normal(keys[11], (D,), jnp.float32), 0.5, 1.5).astype(jnp.bfloat16)
    attn_out_gain = jnp.clip(1.0 + 0.1 * jax.random.normal(keys[12], (D,), jnp.float32), 0.5, 1.5).astype(jnp.bfloat16)
    ffn_in_gain = jnp.clip(1.0 + 0.1 * jax.random.normal(keys[13], (D,), jnp.float32), 0.5, 1.5).astype(jnp.bfloat16)
    ffn_out_gain = jnp.clip(1.0 + 0.1 * jax.random.normal(keys[14], (D,), jnp.float32), 0.5, 1.5).astype(jnp.bfloat16)
    query_gain = jnp.clip(1.0 + 0.15 * jax.random.normal(keys[15], (HD,), jnp.float32), 0.25, 1.75).astype(jnp.bfloat16)
    key_gain = jnp.clip(1.0 + 0.15 * jax.random.normal(keys[16], (HD,), jnp.float32), 0.25, 1.75).astype(jnp.bfloat16)
    return {"tokens": tokens, "out_grad": out_grad, "doc_lengths": doc_lengths, "picture_starts": picture_starts, "q_weight": q_weight, "k_weight": k_weight, "v_weight": v_weight, "out_weight": out_weight, "gate_weight": gate_weight, "up_weight": up_weight, "down_weight": down_weight, "attn_in_gain": attn_in_gain, "attn_out_gain": attn_out_gain, "ffn_in_gain": ffn_in_gain, "ffn_out_gain": ffn_out_gain, "query_gain": query_gain, "key_gain": key_gain}


EPSILON = 1e-06
ROPE_BASE = 1000000.0
PRECISE = lax.Precision.HIGHEST

@jax.custom_vjp
def low(v):
    return lax.optimization_barrier(v.astype(jnp.bfloat16)).astype(jnp.float32)

@jax.custom_vjp
def low_back(v):
    return v

def low_keep(v):
    return (low(v), None)

def low_pass(kept, grad):
    return (grad,)

def back_keep(v):
    return (v, None)

def back_low(kept, grad):
    return (low(grad),)
low.defvjp(low_keep, low_pass)
low_back.defvjp(back_keep, back_low)

def root_norm(values, factor):
    return values * lax.rsqrt(lax.optimization_barrier(jnp.mean(values * values, axis=-1, keepdims=True)) + EPSILON) * factor

def rotary(values, places):
    half_dim = values.shape[-1] // 2
    frequency = ROPE_BASE ** (-2.0 * jnp.arange(half_dim, dtype=jnp.float32) / values.shape[-1])
    angles = places.astype(jnp.float32)[:, None] * frequency[None, :]
    cosine = jnp.cos(angles)
    sine_part = jnp.sin(angles)
    first_half = values[..., :half_dim]
    second_half = values[..., half_dim:]
    return jnp.concatenate([first_half * cosine - second_half * sine_part, second_half * cosine + first_half * sine_part], axis=-1)

def layout(lengths, starts, places):
    doc_ends = jnp.cumsum(lengths).astype(jnp.int32)
    before = places[:, None] >= doc_ends[None, :]
    doc_ids = lax.optimization_barrier(jnp.sum(before.astype(jnp.int32), axis=1)).astype(jnp.int32)
    opening = lax.optimization_barrier(jnp.max(jnp.where(before, doc_ends[None, :], jnp.zeros_like(doc_ends)[None, :]), axis=1)).astype(jnp.int32)
    within = (places - opening).astype(jnp.int32)
    inside = (places[:, None] >= starts[None, :]) & (places[:, None] < starts[None, :] + PIC)
    labels = jnp.arange(1, starts.shape[0] + 1, dtype=jnp.int32)
    pictures = (lax.optimization_barrier(jnp.sum(jnp.where(inside, labels[None, :], jnp.zeros_like(labels)[None, :]), axis=1)) - 1).astype(jnp.int32)
    return (doc_ids, within, pictures)

def allowed_mask(query_places, query_docs, query_pics, key_docs, key_pics):
    key_places = jnp.arange(key_docs.shape[0], dtype=jnp.int32)
    causal = key_places[None, :] <= query_places[:, None]
    shared = (query_pics[:, None] == key_pics[None, :]) & (query_pics[:, None] >= 0)
    return (query_docs[:, None] == key_docs[None, :]) & (causal | shared)

def attend_block(queries, query_places, query_docs, query_pics, key_rows, value_rows, key_docs, key_pics):
    scores = low_back(jnp.einsum('hqd,kd->hqk', queries, key_rows, precision=PRECISE))
    allowed = allowed_mask(query_places, query_docs, query_pics, key_docs, key_pics)
    scores = jnp.where(allowed[None], scores, -1e+30)
    attn_probs = jax.nn.softmax(scores, axis=-1)
    return jnp.einsum('hqk,kd->hqd', low(attn_probs), value_rows, precision=PRECISE)

def block_layer(inputs, lengths, starts, params):
    q_weight, k_weight, v_weight, out_weight, gate_weight, up_weight, down_weight, attn_in_gain, attn_out_gain, ffn_in_gain, ffn_out_gain, query_gain, key_gain = params
    places = jnp.arange(LENGTH, dtype=jnp.int32)
    doc_ids, within, pictures = layout(lengths, starts, places)
    normed = low(root_norm(inputs, attn_in_gain))
    query_raw = low_back(jnp.dot(normed, q_weight, precision=PRECISE))
    query_heads = query_raw.reshape(LENGTH, HEADS, HD).transpose(1, 0, 2)
    queries = low(rotary(root_norm(query_heads, query_gain), within) * HD ** (-0.5))
    key_rows = low(rotary(root_norm(low_back(jnp.dot(normed, k_weight, precision=PRECISE)), key_gain), within))
    value_rows = low(low_back(jnp.dot(normed, v_weight, precision=PRECISE)))
    block_rows = math.gcd(LENGTH, 512)
    block_count = LENGTH // block_rows
    checked = jax.checkpoint(attend_block)

    def one_block(block_item):
        query_blk, place_blk, doc_blk, pic_blk = block_item
        return checked(query_blk, place_blk, doc_blk, pic_blk, key_rows, value_rows, doc_ids, pictures)
    query_blocks = queries.reshape(HEADS, block_count, block_rows, HD).transpose(1, 0, 2, 3)
    mixed = lax.map(one_block, (query_blocks, places.reshape(block_count, block_rows), doc_ids.reshape(block_count, block_rows), pictures.reshape(block_count, block_rows)))
    mixed = mixed.transpose(1, 0, 2, 3).reshape(HEADS, LENGTH, HD)
    attended = low_back(low(mixed)).transpose(1, 0, 2).reshape(LENGTH, HEADS * HD)
    branch = low_back(jnp.dot(attended, out_weight.T, precision=PRECISE))
    middle = inputs + root_norm(branch, attn_out_gain)
    ffn_input = low(root_norm(middle, ffn_in_gain))
    gate_act = low_back(jnp.dot(ffn_input, gate_weight, precision=PRECISE))
    up_act = low_back(jnp.dot(ffn_input, up_weight, precision=PRECISE))
    hidden = low(jax.nn.gelu(gate_act, approximate=True) * up_act)
    branch_two = low_back(jnp.dot(hidden, down_weight.T, precision=PRECISE))
    return middle + root_norm(branch_two, ffn_out_gain)

def reference(tokens, out_grad, doc_lengths, picture_starts, q_weight, k_weight, v_weight, out_weight, gate_weight, up_weight, down_weight, attn_in_gain, attn_out_gain, ffn_in_gain, ffn_out_gain, query_gain, key_gain):
    params = tuple((weight_item.astype(jnp.float32) for weight_item in (q_weight, k_weight, v_weight, out_weight, gate_weight, up_weight, down_weight, attn_in_gain, attn_out_gain, ffn_in_gain, ffn_out_gain, query_gain, key_gain)))
    total_seqs = MICRO * SEQS
    inputs = tokens.astype(jnp.float32).reshape(total_seqs, LENGTH, D)
    flat_lengths = doc_lengths.reshape(total_seqs, DOCS)
    flat_starts = picture_starts.reshape(total_seqs, PICS)

    def forward(layer_inputs, layer_params):

        def scan_step(scan_carry, scan_item):
            seq_tokens, lengths, starts = scan_item
            return (scan_carry, block_layer(seq_tokens, lengths, starts, layer_params))
        return lax.scan(scan_step, jnp.zeros((), jnp.float32), (layer_inputs, flat_lengths, flat_starts))[1]
    output, pullback = jax.vjp(forward, inputs, params)
    input_grad, weight_grads = pullback(out_grad.astype(jnp.float32).reshape(total_seqs, LENGTH, D))
    grad_query, grad_key, grad_value, grad_out, grad_gate, grad_up, grad_down, grad_attn_in, grad_attn_out, grad_ffn_in, grad_ffn_out, grad_query_gain, grad_key_gain = weight_grads
    return (output.reshape(MICRO, SEQS, LENGTH, D).astype(jnp.bfloat16), input_grad.reshape(MICRO, SEQS, LENGTH, D).astype(jnp.bfloat16), grad_query, grad_key, grad_value, grad_out, grad_gate, grad_up, grad_down, grad_attn_in, grad_attn_out, grad_ffn_in, grad_ffn_out, grad_query_gain, grad_key_gain)
```

```python
import jax
import jax.numpy as jnp
from jax import lax
from jax.sharding import Mesh
from jax.sharding import PartitionSpec as P

HD = 256
PIC = 256
EPSILON = 1e-06
ROPE_BASE = 1000000.0
F32 = jnp.float32
BF16 = jnp.bfloat16


def dot(left, right, dims):
    return lax.dot_general(left, right, ((dims[0], dims[1]), ((), ())), preferred_element_type=F32)


def mm(left, right):
    return dot(left, right, ((1,), (0,)))


def mm_nt(left, right):
    return dot(left, right, ((1,), (1,)))


def mm_tn(left, right):
    return dot(left, right, ((0,), (0,)))


def inverse_root(values):
    return lax.rsqrt(jnp.mean(values * values, axis=-1, keepdims=True) + EPSILON)


def norm_back(values, factor, grad):
    root = inverse_root(values)
    scaled = grad * factor
    inner = jnp.mean(values * scaled, axis=-1, keepdims=True)
    grad_values = root * (scaled - values * (root * root * inner))
    return grad_values, jnp.sum(grad * values * root, axis=0)


def turn(values, cosine, sine):
    half = values.shape[-1] // 2
    first = values[..., :half]
    second = values[..., half:]
    return jnp.concatenate([first * cosine - second * sine, second * cosine + first * sine], axis=-1)


def layout(lengths, starts, places):
    doc_ends = jnp.cumsum(lengths)
    before = places[:, None] >= doc_ends[None, :]
    doc_ids = jnp.sum(before.astype(jnp.int32), axis=1)
    opening = jnp.max(jnp.where(before, doc_ends[None, :], 0), axis=1)
    inside = (places[:, None] >= starts[None, :]) & (places[:, None] < starts[None, :] + PIC)
    labels = jnp.arange(1, starts.shape[0] + 1, dtype=jnp.int32)
    pictures = jnp.sum(jnp.where(inside, labels[None, :], 0), axis=1) - 1
    return doc_ids, places - opening, pictures


def shift(values, axis, step):
    size = lax.axis_size(axis)
    return lax.ppermute(values, axis, [(i, (i + step) % size) for i in range(size)])


def gather_rows(own):
    near = [own] + [shift(own, "tensor", k) for k in range(1, lax.axis_size("tensor"))]
    row = jnp.concatenate(near, axis=0)
    rest = [row] + [shift(row, "core", k) for k in range(1, lax.axis_size("core"))]
    return jnp.concatenate(rest, axis=0)


def scatter_rows(parts):
    cores = lax.axis_size("core")
    tensors = lax.axis_size("tensor")
    rows = parts.shape[0] // cores
    total = parts[:rows]
    for k in range(1, cores):
        total = total + shift(parts[k * rows : (k + 1) * rows].astype(BF16), "core", -k).astype(F32)
    rows = rows // tensors
    result = total[:rows]
    for k in range(1, tensors):
        result = result + shift(total[k * rows : (k + 1) * rows].astype(BF16), "tensor", -k).astype(F32)
    return result


def ring_order(count):
    return list(range(0, count, 2)) + list(range(1, count, 2))[::-1]


def ring_pairs(count, way):
    ring = ring_order(count)
    return [(ring[i], ring[(i + way) % count]) for i in range(count)]


def ring_place(place, offset):
    count = lax.axis_size("seq")
    return jnp.array(ring_order(count), jnp.int32)[(place + offset) % count]


def ring_gather(chains, place):
    count = lax.axis_size("seq")
    moving = [block for block, _ in chains]
    spot = ring_place(place, 0)
    full = [
        lax.dynamic_update_slice(
            jnp.zeros((count * b.shape[0],) + b.shape[1:], b.dtype), b, (spot * b.shape[0], 0)
        )
        for b in moving
    ]
    for step in range(1, count):
        for i, (_, way) in enumerate(chains):
            moving[i] = lax.ppermute(moving[i], "seq", ring_pairs(count, way))
            spot = ring_place(place, -way * step)
            full[i] = lax.dynamic_update_slice(full[i], moving[i], (spot * moving[i].shape[0], 0))
    return full


def ring_scatter(chains, place):
    count = lax.axis_size("seq")
    sums = [make(ring_place(place, -way)) for make, way in chains]
    for step in range(1, count):
        for i, (make, way) in enumerate(chains):
            arrived = lax.ppermute(sums[i].astype(BF16), "seq", ring_pairs(count, way))
            sums[i] = arrived.astype(F32) + make(ring_place(place, -way * (step + 1)))
    return sums


def sum_all(values):
    for axis in ("core", "tensor", "seq"):
        size = lax.axis_size(axis)
        hop = 1
        while hop < size:
            values = values + lax.ppermute(values, axis, [(i, i ^ hop) for i in range(size)])
            hop *= 2
    return values


def sum_tensor(values):
    if lax.axis_size("tensor") == 2:
        return values + shift(values, "tensor", 1)
    return lax.psum(values, "tensor")


def body(
    tokens,
    out_grad,
    doc_lengths,
    picture_starts,
    q_weight,
    k_weight,
    v_weight,
    out_weight,
    gate_weight,
    up_weight,
    down_weight,
    attn_in_gain,
    attn_out_gain,
    ffn_in_gain,
    ffn_out_gain,
    query_gain,
    key_gain,
):
    seqs = lax.axis_size("seq")
    cores = lax.axis_size("core")
    tensors = lax.axis_size("tensor")
    s_index = lax.axis_index("seq")
    c_index = lax.axis_index("core")
    t_index = lax.axis_index("tensor")
    micro, per_micro, span, width = tokens.shape
    place = jnp.array([ring_order(seqs).index(i) for i in range(seqs)], jnp.int32)[s_index]
    heads_here = q_weight.shape[1] // HD
    split_heads = heads_here > 1
    assert heads_here == (cores if split_heads else 1)
    own_feats = k_weight.shape[0]

    if split_heads:
        q_block, out_block = (
            lax.all_to_all(w, "core", split_axis=1, concat_axis=0, tiled=True) for w in (q_weight, out_weight)
        )
    else:
        q_block, out_block = (lax.all_gather(w, "core", axis=0, tiled=True) for w in (q_weight, out_weight))
    gains = jnp.concatenate([attn_in_gain, attn_out_gain, ffn_in_gain, ffn_out_gain, query_gain, key_gain])
    gain_row = jnp.pad(gains[None, :], ((0, 7), (0, 2 * HD - gains.shape[0])))
    kv_block = jnp.concatenate([jnp.concatenate([k_weight, v_weight], axis=1), gain_row], axis=0)
    q_out, kv_mine = ring_gather([(jnp.concatenate([q_block, out_block], axis=1), 1), (kv_block, -1)], place)
    q_full = q_out[:, :HD]
    out_full = q_out[:, HD:]
    kv_all = lax.all_gather(kv_mine.reshape(seqs, -1, 2 * HD), "core", axis=1)
    kv_full = kv_all[:, :, :own_feats].reshape(width, 2 * HD)
    gain_all = kv_all[:, :, own_feats].astype(F32)
    gain_sizes = [own_feats] * 4 + [query_gain.shape[0]] * 2
    gain_ends = [sum(gain_sizes[: i + 1]) for i in range(6)]
    g_in, g_ao, g_fi, g_fo, g_q, g_k = (
        gain_all[:, :, end - size : end].reshape(1, -1) for end, size in zip(gain_ends, gain_sizes)
    )
    qkv_full = jnp.concatenate([q_full, kv_full], axis=1)

    gate_block, up_block, down_block = (
        lax.all_to_all(w, "core", split_axis=1, concat_axis=0, tiled=True)
        for w in (gate_weight, up_weight, down_weight)
    )
    gate_full, up_full = ring_gather([(gate_block, 1), (up_block, -1)], place)
    half = down_block.shape[0] // 2
    down_low, down_high = ring_gather([(down_block[:half], 1), (down_block[half:], -1)], place)
    hidden_here = gate_block.shape[1]
    down_full = jnp.concatenate(
        [down_low.reshape(seqs, half, hidden_here), down_high.reshape(seqs, half, hidden_here)], axis=1
    ).reshape(width, hidden_here)

    def to_rows(values):
        moved = lax.all_to_all(values.reshape(seqs, span, width), "seq", split_axis=0, concat_axis=0, tiled=True)
        return moved.reshape(seqs * span, width)

    def from_rows(values):
        moved = lax.all_to_all(values.reshape(seqs, span, width), "seq", split_axis=0, concat_axis=0, tiled=True)
        return moved.reshape(micro, per_micro, span, width)

    x = to_rows(tokens).astype(F32)
    cotangent = to_rows(out_grad).astype(F32)

    steps = jnp.arange(cores, dtype=jnp.int32)
    owner_core = ((c_index - steps) % cores)[:, None, None, None]
    owner_tensor = ((t_index - jnp.arange(tensors, dtype=jnp.int32)) % tensors)[None, :, None, None]
    block_index = jnp.arange(seqs, dtype=jnp.int32)[None, None, :, None]
    inner = jnp.arange(span, dtype=jnp.int32)[None, None, None, :]
    places = (((block_index * cores + owner_core) * tensors + owner_tensor) * span + inner).reshape(-1)
    docs, within, pics = layout(
        doc_lengths.reshape(seqs, -1)[s_index], picture_starts.reshape(seqs, -1)[s_index], places
    )
    frequency = ROPE_BASE ** (-2.0 * jnp.arange(HD // 2, dtype=F32) / HD)
    angles = within.astype(F32)[:, None] * frequency[None, :]
    cosine = jnp.cos(angles)
    sine = jnp.sin(angles)
    rows = places.shape[0]
    q_rows = rows if split_heads else rows // cores

    a_own = (x * inverse_root(x) * g_in).astype(BF16)
    a_all = gather_rows(a_own)
    raw = mm(a_all, qkv_full)
    q_raw = raw[:q_rows, :HD]
    k_raw = raw[:, HD : 2 * HD]
    value = raw[:, 2 * HD :].astype(BF16)
    scale = HD ** (-0.5)
    query = (turn(q_raw * inverse_root(q_raw) * g_q, cosine[:q_rows], sine[:q_rows]) * scale).astype(BF16)
    key = turn(k_raw * inverse_root(k_raw) * g_k, cosine, sine).astype(BF16)
    allowed = (docs[:q_rows, None] == docs[None, :]) & (
        (places[None, :] <= places[:q_rows, None])
        | ((pics[:q_rows, None] == pics[None, :]) & (pics[:q_rows, None] >= 0))
    )
    scores = jnp.where(allowed, mm_nt(query, key), -1e30)
    top = jnp.max(scores, axis=-1, keepdims=True)
    log_total = top + jnp.log(jnp.sum(jnp.exp(scores - top), axis=-1, keepdims=True))
    prob = jnp.exp(scores - log_total)
    attended = mm(prob.astype(BF16), value).astype(BF16)
    branch_part = mm_nt(attended, out_full)
    if q_rows != rows:
        branch_part = jnp.pad(branch_part, ((0, rows - q_rows), (0, 0)))
    branch = scatter_rows(branch_part)

    middle = x + branch * inverse_root(branch) * g_ao
    f_own = (middle * inverse_root(middle) * g_fi).astype(BF16)
    f_all = gather_rows(f_own)
    gate_act = mm(f_all, gate_full)
    up_act = mm(f_all, up_full)
    gelu, pull_gelu = jax.vjp(lambda v: jax.nn.gelu(v, approximate=True), gate_act)
    hidden = (gelu * up_act).astype(BF16)
    second = scatter_rows(mm_nt(hidden, down_full))
    output = middle + second * inverse_root(second) * g_fo

    grad_second, grad_fo = norm_back(second, g_fo, cotangent)
    de_all = gather_rows(grad_second.astype(BF16))
    grad_hidden = mm(de_all, down_full)
    up_grad = (grad_hidden * gelu).astype(BF16)
    gate_grad = pull_gelu(grad_hidden * up_act)[0].astype(BF16)

    def blocks(left, right, first, count):
        left_t = left.T

        def make(spot):
            start = spot * (left_t.shape[0] // seqs) + first
            return mm(lax.dynamic_slice_in_dim(left_t, start, count, 0), right)

        return make

    feats = width // seqs
    down_low, down_high = ring_scatter(
        [(blocks(de_all, hidden, 0, half), 1), (blocks(de_all, hidden, half, half), -1)], place
    )
    down_sum = jnp.concatenate([down_low, down_high], axis=0)
    gate_sum, up_sum = ring_scatter(
        [(blocks(f_all, gate_grad, 0, feats), 1), (blocks(f_all, up_grad, 0, feats), -1)], place
    )
    grad_f = scatter_rows(mm_nt(gate_grad, gate_full) + mm_nt(up_grad, up_full))
    back_middle, grad_fi = norm_back(middle, g_fi, grad_f)
    grad_middle = cotangent + back_middle

    grad_branch, grad_ao = norm_back(branch, g_ao, grad_middle)
    dr_all = gather_rows(grad_branch.astype(BF16))
    grad_attended = mm(dr_all[:q_rows], out_full).astype(BF16)
    grad_prob = mm_nt(grad_attended, value)
    grad_scores = (prob * (grad_prob - jnp.sum(prob * grad_prob, axis=-1, keepdims=True))).astype(BF16)
    grad_query = mm(grad_scores, key)
    grad_key = mm_tn(grad_scores, query)
    grad_value = mm_tn(prob.astype(BF16), grad_attended)
    back_query, grad_gq = norm_back(q_raw, g_q, turn(grad_query * scale, cosine[:q_rows], -sine[:q_rows]))
    back_key, grad_gk = norm_back(k_raw, g_k, turn(grad_key, cosine, -sine))
    query_low = back_query.astype(BF16)
    kv_low = jnp.concatenate([back_key, grad_value], axis=1).astype(BF16)

    out_sum, q_sum = ring_scatter(
        [
            (blocks(dr_all[:q_rows], attended, 0, feats), 1),
            (blocks(a_all[:q_rows], query_low, 0, feats), -1),
        ],
        place,
    )
    kv_parts = mm_tn(a_all, kv_low).reshape(seqs, cores, own_feats, 2 * HD)
    kv_core = lax.dynamic_index_in_dim(kv_parts, c_index, 1, keepdims=False)
    for k in range(1, cores):
        going = lax.dynamic_index_in_dim(kv_parts, (c_index + k) % cores, 1, keepdims=False)
        kv_core = kv_core + shift(going.astype(BF16), "core", k).astype(F32)
    kv_sum = ring_scatter(
        [(lambda spot: lax.dynamic_index_in_dim(kv_core, spot, 0, keepdims=False), 1)], place
    )[0]
    kv_sum = sum_tensor(kv_sum)

    query_part = mm_nt(query_low, q_full)
    if q_rows != rows:
        query_part = jnp.pad(query_part, ((0, rows - q_rows), (0, 0)))
    grad_a = scatter_rows(query_part + mm_nt(kv_low, kv_full))
    back_x, grad_in = norm_back(x, g_in, grad_a)
    input_grad = grad_middle + back_x

    def to_owner(values):
        return lax.all_to_all(values, "core", split_axis=0, concat_axis=1, tiled=True)

    if split_heads:
        q_grad, out_grad_w = to_owner(q_sum), to_owner(out_sum)
    else:
        q_grad, out_grad_w = (
            lax.psum_scatter(v, "core", scatter_dimension=0, tiled=True) for v in (q_sum, out_sum)
        )
    gain_grads = (grad_in, grad_ao, grad_fi, grad_fo, grad_gq, grad_gk)
    packed = jnp.concatenate([g.reshape(seqs * cores, -1) for g in gain_grads], axis=1)
    shape = packed.shape
    packed = sum_all(packed.reshape(-1, 128)).reshape(shape)
    mine = lax.dynamic_index_in_dim(packed, s_index * cores + c_index, 0, keepdims=False)
    gain_out = tuple(mine[end - size : end] for end, size in zip(gain_ends, gain_sizes))
    return (
        from_rows(output.astype(BF16)),
        from_rows(input_grad.astype(BF16)),
        q_grad,
        kv_sum[:, :HD],
        kv_sum[:, HD:],
        out_grad_w,
        to_owner(gate_sum),
        to_owner(up_sum),
        to_owner(down_sum),
    ) + gain_out


def solution(mesh):
    def run(tokens, *rest):
        seqs = tokens.shape[0] * tokens.shape[1]
        wide, tensor = mesh.shape["wide"], mesh.shape["tensor"]
        fine = Mesh(mesh.devices.reshape(seqs, wide // seqs, tensor), ("seq", "core", "tensor"))
        acts = P(None, None, ("seq", "core", "tensor"), None)
        both = P(("seq", "core"), "tensor")
        rows = P(("seq", "core"), None)
        vector = P(("seq", "core"))
        weights = (both, rows, rows, both, both, both, both) + (vector,) * 6
        return jax.shard_map(
            body,
            mesh=fine,
            in_specs=(acts, acts, P(), P()) + weights,
            out_specs=(acts, acts) + weights,
            check_vma=False,
        )(tokens, *rest)

    return run
```

```python
import functools

import jax
import jax.numpy as jnp
from jax import lax
from jax.experimental import pallas as pl
from jax.experimental.pallas import tpu as pltpu
from jax.sharding import Mesh
from jax.sharding import PartitionSpec as P

HD = 256
PIC = 256
EPSILON = 1e-06
ROPE_BASE = 1000000.0
SCALE = HD ** (-0.5)
TILE = 256
F32 = jnp.float32
BF16 = jnp.bfloat16


def dot(left, right, dims):
    return lax.dot_general(left, right, ((dims[0], dims[1]), ((), ())), preferred_element_type=F32)


def mm(left, right):
    return dot(left, right, ((1,), (0,)))


def mm_nt(left, right):
    return dot(left, right, ((1,), (1,)))


def mm_tn(left, right):
    return dot(left, right, ((0,), (0,)))


def inverse_root(values):
    return lax.rsqrt(jnp.mean(values * values, axis=-1, keepdims=True) + EPSILON)


def norm_back(values, factor, grad):
    root = inverse_root(values)
    scaled = grad * factor
    inner = jnp.mean(values * scaled, axis=-1, keepdims=True)
    grad_values = root * (scaled - values * (root * root * inner))
    return grad_values, jnp.sum(grad * (values * root), axis=0, keepdims=True)


def turn(values, cosine, sine):
    half = values.shape[-1] // 2
    first = values[..., :half]
    second = values[..., half:]
    return jnp.concatenate([first * cosine - second * sine, second * cosine + first * sine], axis=-1)


def gelu_parts(v):
    c = (2.0 / jnp.pi) ** 0.5
    square = v * v
    t = jnp.tanh(c * v * (1.0 + 0.044715 * square))
    value = 0.5 * v * (1.0 + t)
    slope = 0.5 * (1.0 + t) + 0.5 * v * (1.0 - t * t) * (c * (1.0 + 0.134145 * square))
    return value, slope


def call(kernel, outs, ins, scratch=(), mib=48, flops=0, moved=0, **more):
    return pl.pallas_call(
        kernel,
        out_shape=outs,
        scratch_shapes=list(scratch),
        compiler_params=pltpu.CompilerParams(vmem_limit_bytes=mib << 20),
        cost_estimate=pl.CostEstimate(flops=0, bytes_accessed=1, transcendentals=0),
        **more,
    )(*ins)


def small_call(kernel, outs, ins, **more):
    vmem = pl.BlockSpec(memory_space=pltpu.VMEM)
    moved = sum(v.size * v.dtype.itemsize for v in (*ins, *outs))
    return call(
        kernel, outs, ins, in_specs=[vmem] * len(ins), out_specs=[vmem] * len(outs), moved=moved, **more
    )


def struct(shape, kind):
    return jax.ShapeDtypeStruct(shape, kind)


def total_of(refs):
    total = refs[0][...].astype(F32)
    for ref in refs[1:]:
        total = total + ref[...].astype(F32)
    return total


def start_kernel(x_ref, gain_ref, a_ref):
    x = x_ref[...].astype(F32)
    a_ref[...] = (x * inverse_root(x) * gain_ref[...]).astype(BF16)


def middle_kernel(count, *refs):
    x_ref, g_ao, g_fi = refs[count : count + 3]
    r_ref, mid_ref, f_ref = refs[count + 3 :]
    r = total_of(refs[:count])
    mid = x_ref[...].astype(F32) + r * inverse_root(r) * g_ao[...]
    r_ref[...] = r
    mid_ref[...] = mid
    f_ref[...] = (mid * inverse_root(mid) * g_fi[...]).astype(BF16)


def close_kernel(count, *refs):
    mid_ref, cot_ref, g_fo = refs[count : count + 3]
    out_ref, de_ref, gain_ref = refs[count + 3 :]
    e = total_of(refs[:count])
    cot = cot_ref[...].astype(F32)
    out_ref[...] = (mid_ref[...] + e * inverse_root(e) * g_fo[...]).astype(BF16)
    de, gain = norm_back(e, g_fo[...], cot)
    de_ref[...] = de.astype(BF16)
    gain_ref[...] = gain


def turn_kernel(count, *refs):
    mid_ref, cot_ref, r_ref, g_fi, g_ao = refs[count : count + 5]
    dmid_ref, dr_ref, gain_fi, gain_ao = refs[count + 5 :]
    back, gain = norm_back(mid_ref[...], g_fi[...], total_of(refs[:count]))
    gain_fi[...] = gain
    dmid = cot_ref[...].astype(F32) + back
    dmid_ref[...] = dmid
    dr, gain = norm_back(r_ref[...], g_ao[...], dmid)
    gain_ao[...] = gain
    dr_ref[...] = dr.astype(BF16)


def last_kernel(count, *refs):
    x_ref, dmid_ref, g_in = refs[count : count + 3]
    dx_ref, gain_ref = refs[count + 3 :]
    back, gain = norm_back(x_ref[...].astype(F32), g_in[...], total_of(refs[:count]))
    dx_ref[...] = (dmid_ref[...] + back).astype(BF16)
    gain_ref[...] = gain


def attend_kernel(count, q_blocks, *refs):
    a_refs = refs[:count]
    qkv, out_w, cosine, sine, g_q, g_k, meta_q, meta_k = refs[count : count + 8]
    o_ref, prob_ref, raw_ref, q_ref, k_ref, v_ref = refs[count + 8 : count + 14]
    r_refs = refs[count + 14 :]
    size = a_refs[0].shape[0]
    for i, a_ref in enumerate(a_refs):
        rows = slice(i * size, (i + 1) * size)
        raw = mm(a_ref[...], qkv[...])
        raw_ref[rows] = raw[:, : 2 * HD].astype(BF16)
        cos, sin = cosine[rows], sine[rows]
        query, key = raw[:, :HD], raw[:, HD : 2 * HD]
        q_ref[rows] = (turn(query * inverse_root(query) * g_q[...], cos, sin) * SCALE).astype(BF16)
        k_ref[rows] = turn(key * inverse_root(key) * g_k[...], cos, sin).astype(BF16)
        v_ref[rows] = raw[:, 2 * HD :].astype(BF16)
    key_doc, key_place, key_pic = meta_k[0:1], meta_k[1:2], meta_k[2:3]
    for n, i in enumerate(q_blocks):
        rows = slice(i * size, (i + 1) * size)
        done = slice(n * size, (n + 1) * size)
        scores = mm_nt(q_ref[rows], k_ref[...])
        doc, place, pic = meta_q[rows, 0:1], meta_q[rows, 1:2], meta_q[rows, 2:3]
        allowed = (doc == key_doc) & ((key_place <= place) | ((pic == key_pic) & (pic >= 0)))
        scores = jnp.where(allowed, scores, -1e30)
        weight = jnp.exp(scores - jnp.max(scores, axis=-1, keepdims=True))
        prob = (weight * (1.0 / jnp.sum(weight, axis=-1, keepdims=True))).astype(BF16)
        prob_ref[done] = prob
        o = mm(prob, v_ref[...]).astype(BF16)
        o_ref[done] = o
        r_refs[n][...] = mm_nt(o, out_w[...]).astype(BF16)


def attend_back_kernel(count, q_blocks, total, *refs):
    dr_refs = refs[:count]
    prob_ref, raw_ref, q_ref, k_ref, v_ref, qkv, out_w, cosine, sine, g_q, g_k = refs[count : count + 11]
    grad_ref, gain_q, gain_k = refs[count + 11 : count + 14]
    da_refs = refs[count + 14 : count + 14 + total]
    dk_ref, dv_ref = refs[count + 14 + total :]
    size = dr_refs[0].shape[0]
    if len(q_blocks) != total:
        grad_ref[:, :HD] = jnp.zeros((size * total, HD), BF16)
    sum_q = jnp.zeros((1, HD), F32)
    sum_k = jnp.zeros((1, HD), F32)
    for n, i in enumerate(q_blocks):
        rows = slice(i * size, (i + 1) * size)
        done = slice(n * size, (n + 1) * size)
        do = mm(dr_refs[n][...], out_w[...]).astype(BF16)
        prob_low = prob_ref[done]
        prob = prob_low.astype(F32)
        dprob = mm_nt(do, v_ref[...])
        ds = (prob * (dprob - jnp.sum(prob * dprob, axis=-1, keepdims=True))).astype(BF16)
        dq = mm(ds, k_ref[...])
        dk = mm_tn(ds, q_ref[rows])
        dv = mm_tn(prob_low, do)
        if n == 0:
            dk_ref[...] = dk
            dv_ref[...] = dv
        else:
            dk_ref[...] += dk
            dv_ref[...] += dv
        raw = raw_ref[rows, :HD].astype(F32)
        back, gain = norm_back(raw, g_q[...], turn(dq * SCALE, cosine[rows], -sine[rows]))
        grad_ref[rows, :HD] = back.astype(BF16)
        sum_q = sum_q + gain
    for i in range(total):
        rows = slice(i * size, (i + 1) * size)
        raw = raw_ref[rows, HD:].astype(F32)
        back, gain = norm_back(raw, g_k[...], turn(dk_ref[rows], cosine[rows], -sine[rows]))
        grad_ref[rows, HD : 2 * HD] = back.astype(BF16)
        grad_ref[rows, 2 * HD :] = dv_ref[rows].astype(BF16)
        sum_k = sum_k + gain
        da_refs[i][...] = mm_nt(grad_ref[rows], qkv[...]).astype(BF16)
    gain_q[...] = sum_q
    gain_k[...] = sum_k


def hidden_kernel(count, *refs):
    gate_w, up_w, keep_gate, keep_up, hid_ref = refs[count:]
    size = refs[0].shape[0]
    for i in range(count):
        rows = slice(i * size, (i + 1) * size)
        gate = mm(refs[i][...], gate_w[...])
        up = mm(refs[i][...], up_w[...])
        value, slope = gelu_parts(gate)
        keep_gate[rows] = (up * slope).astype(BF16)
        keep_up[rows] = value.astype(BF16)
        hid_ref[rows] = (value * up).astype(BF16)


def down_kernel(hid_ref, down_w, *outs):
    size = outs[0].shape[0]
    part = mm_nt(hid_ref[...], down_w[...]).astype(BF16)
    for i, out in enumerate(outs):
        out[...] = part[i * size : (i + 1) * size]


def hidden_back_kernel(count, *refs):
    keep_gate, keep_up, gate_w, up_w, down_w, dgate_ref, dup_ref = refs[count : count + 7]
    df_refs = refs[count + 7 :]
    size = refs[0].shape[0]
    for i in range(count):
        rows = slice(i * size, (i + 1) * size)
        dhid = mm(refs[i][...], down_w[...])
        dgate_ref[rows] = (dhid * keep_gate[rows].astype(F32)).astype(BF16)
        dup_ref[rows] = (dhid * keep_up[rows].astype(F32)).astype(BF16)
        df_refs[i][...] = (mm_nt(dgate_ref[rows], gate_w[...]) + mm_nt(dup_ref[rows], up_w[...])).astype(BF16)


def hidden_forward(pieces, gate_w, up_w):
    size, hidden = pieces[0].shape[0], gate_w.shape[1]
    return small_call(
        functools.partial(hidden_kernel, len(pieces)),
        [struct((len(pieces) * size, hidden), BF16)] * 3,
        (*pieces, gate_w, up_w),
        mib=24,
    )


def down_forward(hid, down_w, count):
    shape = hid.shape[0] // count, down_w.shape[0]
    return small_call(down_kernel, [struct(shape, BF16)] * count, (hid, down_w), mib=24)


def hidden_backward(pieces, keep_gate, keep_up, gate_w, up_w, down_w):
    size, width = pieces[0].shape
    count, hidden = len(pieces), gate_w.shape[1]
    return small_call(
        functools.partial(hidden_back_kernel, count),
        [struct((count * size, hidden), BF16)] * 2 + [struct((size, width), BF16)] * count,
        (*pieces, keep_gate, keep_up, gate_w, up_w, down_w),
        mib=24,
    )


def outer_kernel(groups, spots, *refs):
    count = spots.shape[0]
    outs, whole = refs[-1 - count : -1], refs[-1]
    feats = whole.shape[0] // count
    used, column = 0, 0
    for lefts, rights in groups:
        left = jnp.concatenate([r[...] for r in refs[used : used + lefts]], axis=0)
        right = jnp.concatenate([r[...] for r in refs[used + lefts : used + lefts + rights]], axis=0)
        whole[:, column : column + right.shape[1]] = mm_tn(left, right).astype(BF16)
        used, column = used + lefts + rights, column + right.shape[1]
    for k, out in enumerate(outs):
        first = pl.multiple_of(spots[(k + 1) % count] * feats, 16)
        out[...] = whole[pl.ds(first, feats), :]


def outer(products, spots):
    count = spots.shape[0]
    width = products[0][0][0].shape[1]
    total = sum(right[0].shape[1] for _, right in products)
    ins = [v for left, right in products for v in (*left, *right)]
    vmem = pl.BlockSpec(memory_space=pltpu.VMEM)
    return call(
        functools.partial(outer_kernel, [(len(left), len(right)) for left, right in products]),
        [struct((width // count, total), BF16)] * count,
        (spots, *ins),
        scratch=[pltpu.VMEM((width, total), BF16)],
        in_specs=[pl.BlockSpec(memory_space=pltpu.SMEM)] + [vmem] * len(ins),
        out_specs=[vmem] * count,
        mib=32,
    )


def layout(lengths, starts, places):
    doc_ends = jnp.cumsum(lengths)
    before = places[:, None] >= doc_ends[None, :]
    doc_ids = jnp.sum(before.astype(jnp.int32), axis=1)
    opening = jnp.max(jnp.where(before, doc_ends[None, :], 0), axis=1)
    inside = (places[:, None] >= starts[None, :]) & (places[:, None] < starts[None, :] + PIC)
    labels = jnp.arange(1, starts.shape[0] + 1, dtype=jnp.int32)
    pictures = jnp.sum(jnp.where(inside, labels[None, :], 0), axis=1) - 1
    return doc_ids, places - opening, pictures


def shift(values, axis, step):
    size = lax.axis_size(axis)
    return lax.ppermute(values, axis, [(i, (i + step) % size) for i in range(size)])


def gather_rows(own):
    across = [own] + [shift(own, "tensor", k) for k in range(1, lax.axis_size("tensor"))]
    return [[p] + [shift(p, "core", k) for k in range(1, lax.axis_size("core"))] for p in across]


def scatter_rows(parts):
    result, sent = [], []
    for k in list(range(1, len(parts))) + [0]:
        first = [parts[k][0]] + [shift(p, "core", -j) for j, p in enumerate(parts[k]) if j]
        if k:
            total = first[0].astype(F32)
            for p in first[1:]:
                total = total + p.astype(F32)
            sent.append(total.astype(BF16))
            result.append(shift(sent[-1], "tensor", -k))
        else:
            result.extend(first)
    return result, sent


def ring_order(count):
    return list(range(0, count, 2)) + list(range(1, count, 2))[::-1]


def ring_spots():
    count = lax.axis_size("seq")
    ring = ring_order(count)
    table = [
        [[ring[(ring.index(i) - way * k) % count] for k in range(count)] for i in range(count)] for way in (1, -1)
    ]
    line = jnp.array(table, jnp.int32).reshape(2 * count, count)
    row = (lax.axis_index("core") % 2) * count + lax.axis_index("seq")
    line = lax.dynamic_index_in_dim(line, row, 0, keepdims=False, allow_negative_indices=False)
    return line, [line[k] for k in range(count)]


def together(values, *others):
    return lax.optimization_barrier((tuple(values), others))[0]


def hop(values):
    count, cores = lax.axis_size("seq"), lax.axis_size("core")
    ring = ring_order(count)
    pairs = [
        (ring[i] * cores + c, ring[(i + (-1) ** (c % 2)) % count] * cores + c)
        for i in range(count)
        for c in range(cores)
    ]
    return lax.ppermute(values, ("seq", "core"), pairs)


def put(full, block, row, spot):
    return lax.dynamic_update_slice(full, block[None], (spot, row, 0), allow_negative_indices=False)


def pick(array, spot, axis):
    return lax.dynamic_index_in_dim(array, spot, axis, keepdims=False, allow_negative_indices=False)


class RingSum:
    def __init__(self, blocks):
        self.blocks, self.hops = blocks, 0
        self.sum = blocks[0]

    def left(self):
        return len(self.blocks) - 1 - self.hops

    def step(self):
        self.hops += 1
        total = hop(self.sum).astype(F32) + self.blocks[self.hops].astype(F32)
        self.sum = total if self.left() == 0 else total.astype(BF16)

    def wait(self, *others):
        (self.sum,) = together([self.sum], *others)


def meet(rings, *others):
    values = [ring.sum for ring in rings]
    for ring in rings:
        ring.wait(*values, *others)


def exchanges():
    hops = []
    for axis in ("core", "tensor", "seq"):
        distance = 1
        while distance < lax.axis_size(axis):
            hops.append((axis, distance))
            distance *= 2
    return hops


def exchange(values, axis, distance):
    return values + lax.ppermute(values, axis, [(i, i ^ distance) for i in range(lax.axis_size(axis))])


def sum_tensor(values):
    if lax.axis_size("tensor") == 2:
        return values + shift(values, "tensor", 1)
    return lax.psum(values, "tensor")


def body(
    tokens,
    out_grad,
    doc_lengths,
    picture_starts,
    q_weight,
    k_weight,
    v_weight,
    out_weight,
    gate_weight,
    up_weight,
    down_weight,
    attn_in_gain,
    attn_out_gain,
    ffn_in_gain,
    ffn_out_gain,
    query_gain,
    key_gain,
):
    seqs = lax.axis_size("seq")
    cores = lax.axis_size("core")
    tensors = lax.axis_size("tensor")
    s_index = lax.axis_index("seq")
    c_index = lax.axis_index("core")
    t_index = lax.axis_index("tensor")
    micro, per_micro, span, width = tokens.shape
    split_heads = q_weight.shape[1] > HD
    assert q_weight.shape[1] == HD * (cores if split_heads else 1)
    own_feats = k_weight.shape[0]
    feats = own_feats * cores
    hidden_here = gate_weight.shape[1] // cores
    hidden = -(-hidden_here // TILE) * TILE

    def to_columns(arrays, padded):
        parts = [w.reshape(own_feats, cores, -1).transpose(1, 0, 2) for w in arrays]
        parts = [jnp.pad(p, ((0, 0), (0, 0), (0, padded - p.shape[2]))) for p in parts]
        moved = lax.all_to_all(jnp.concatenate(parts, axis=2), "core", split_axis=0, concat_axis=0, tiled=True)
        moved = moved.reshape(feats, -1)
        return [moved[:, i * padded : (i + 1) * padded] for i in range(len(arrays))]

    def to_rows(values):
        moved = lax.all_to_all(values.reshape(seqs, span, width), "seq", split_axis=0, concat_axis=0, tiled=True)
        return moved.reshape(seqs * span, width)

    def from_rows(values):
        moved = lax.all_to_all(values.reshape(seqs, span, width), "seq", split_axis=0, concat_axis=0, tiled=True)
        return moved.reshape(micro, per_micro, span, width)

    spot_line, spots = ring_spots()
    gains = (attn_in_gain, attn_out_gain, ffn_in_gain, ffn_out_gain, query_gain, key_gain)
    gain_sizes = [v.shape[0] for v in gains]
    gain_ends = [sum(gain_sizes[: i + 1]) for i in range(6)]
    gain_row = sum(jnp.pad(v, (e - n, 2 * HD - e)) for v, e, n in zip(gains, gain_ends, gain_sizes))
    gain_row = jnp.pad(gain_row[None, :], ((0, -(own_feats + 1) % 16), (0, 0)))
    kv_block = jnp.concatenate([jnp.concatenate([k_weight, v_weight], axis=1), gain_row], axis=0)
    some = jnp.concatenate([q_weight, out_weight], axis=1)
    some = jnp.concatenate([kv_block, jnp.pad(some, ((0, kv_block.shape[0] - own_feats), (0, 0)))], axis=1)
    moving = some
    some = put(jnp.zeros((seqs,) + some.shape, BF16), some, 0, spots[0])
    x = to_rows(tokens)
    for step in range(1, seqs):
        if step == 3:
            moving = together([moving], x)[0]
        moving = hop(moving)
        some = put(some, moving, 0, spots[step])
    early = moving
    if cores == 2:
        other = shift(some, "core", 1)
        some = jnp.where(c_index == 0, jnp.stack([some, other], axis=1), jnp.stack([other, some], axis=1))
    else:
        some = lax.all_gather(some, "core", axis=1)
    some = some.reshape((seqs * cores,) + some.shape[2:])
    gain_all = some[:, own_feats].astype(F32).reshape(seqs, cores, -1)
    first = 2 * HD + (c_index * HD if split_heads else 0)

    def columns(start, many):
        return lax.dynamic_slice(
            some, (0, 0, start), (seqs * cores, own_feats, many), allow_negative_indices=False
        ).reshape(width, many)

    q_full = columns(first, HD)
    out_full = columns(first + q_weight.shape[1], HD)
    qkv_full = jnp.concatenate([q_full, columns(0, 2 * HD)], axis=1)
    g_in, g_ao, g_fi, g_fo, g_q, g_k = (
        gain_all[:, :, end - size : end].reshape(1, -1) for end, size in zip(gain_ends, gain_sizes)
    )

    size = seqs * span
    group = cores * tensors
    rows = size * group

    owner_tensor = ((t_index - jnp.arange(tensors, dtype=jnp.int32)) % tensors)[:, None, None, None]
    owner_core = ((c_index - jnp.arange(cores, dtype=jnp.int32)) % cores)[None, :, None, None]
    block_index = jnp.arange(seqs, dtype=jnp.int32)[None, None, :, None]
    inner = jnp.arange(span, dtype=jnp.int32)[None, None, None, :]
    places = (((block_index * cores + owner_core) * tensors + owner_tensor) * span + inner).reshape(-1)
    docs, within, pics = layout(
        *(pick(v.reshape(seqs, -1), s_index, 0) for v in (doc_lengths, picture_starts)), places
    )
    frequency = ROPE_BASE ** (-2.0 * jnp.arange(HD // 2, dtype=F32) / HD)
    angles = within.astype(F32)[:, None] * frequency[None, :]
    cosine = jnp.cos(angles)
    sine = jnp.sin(angles)
    meta = [docs, places, pics] + [jnp.zeros_like(docs)] * 5
    meta_q = jnp.stack(meta, axis=1)
    meta_k = jnp.stack(meta, axis=0)
    q_blocks = list(range(group)) if split_heads else [k * cores for k in range(tensors)]
    q_count = len(q_blocks)
    block = struct((size, width), BF16)
    vector = struct((1, width), F32)

    def flat(lists):
        return [p for line in lists for p in line]

    def by_tensor(pieces):
        return [pieces[k * cores : (k + 1) * cores] for k in range(tensors)]

    (a_own,) = small_call(start_kernel, [block], (x, g_in))
    a_all = flat(gather_rows(a_own))
    low_rows = struct((rows, HD), BF16)
    o, prob, raw, query, key, value, *r_parts = small_call(
        functools.partial(attend_kernel, group, q_blocks),
        [struct((q_count * size, HD), BF16), struct((q_count * size, rows), BF16), struct((rows, 2 * HD), BF16)]
        + [low_rows] * 3
        + [block] * q_count,
        (*a_all, qkv_full, out_full, cosine, sine, g_q, g_k, meta_q, meta_k),
        flops=2 * rows * width * 3 * HD + 2 * q_count * size * HD * (2 * rows + width),
    )
    if q_count != group:
        spread = [jnp.zeros((size, width), BF16)] * group
        for i, part in zip(q_blocks, r_parts):
            spread[i] = part
        r_parts = spread
    shares, _ = scatter_rows(by_tensor(r_parts))

    branch, middle, f_own = small_call(
        functools.partial(middle_kernel, len(shares)),
        [struct((size, width), F32)] * 2 + [block],
        (*shares, x, g_ao, g_fi),
    )
    f_all = gather_rows(f_own)

    blocks = to_columns([gate_weight, up_weight, down_weight], hidden)
    moving = together(blocks, early)
    fulls = [put(jnp.zeros((seqs, feats, hidden), BF16), v, 0, spots[0]) for v in moving]
    ahead = {2: a_own, 4: o, 6: f_own}
    for step in range(1, seqs):
        if step in ahead:
            moving = together(moving, ahead[step])
        moving = [hop(v) for v in moving]
        fulls = [put(full, v, 0, spots[step]) for full, v in zip(fulls, moving)]
    gate_full, up_full, down_full = fulls
    gate_full, up_full, down_full = (w.reshape(width, hidden) for w in (gate_full, up_full, down_full))
    gates, ups, hids = zip(*(hidden_forward(line, gate_full, up_full) for line in f_all))
    cotangent = to_rows(together([out_grad], *moving)[0])
    e_parts = [None] * tensors
    for k in list(range(1, tensors)) + [0]:
        e_parts[k] = down_forward(hids[k] if k else together([hids[k]], cotangent)[0], down_full, cores)
    shares, _ = scatter_rows(e_parts)
    output, de_own, gain_fo = small_call(
        functools.partial(close_kernel, len(shares)),
        [block, block, vector],
        (*shares, middle, cotangent, g_fo),
    )

    de_all = gather_rows(de_own)
    downs = RingSum(outer([(flat(de_all), hids)], spot_line))
    dgates, dups, df_parts = [None] * tensors, [None] * tensors, [None] * tensors
    for k in list(range(1, tensors)) + [0]:
        dgates[k], dups[k], *df_parts[k] = hidden_backward(
            together(de_all[k], downs.sum), gates[k], ups[k], gate_full, up_full, down_full
        )
        downs.step()
        downs.wait(dgates[k])
    output = from_rows(together([output], downs.sum)[0])
    shares, _ = scatter_rows(df_parts)
    pieces = flat(f_all)
    bigs = RingSum(outer([(pieces, together(dgates, downs.sum)), (pieces, dups)], spot_line))
    downs.step()
    rings = [bigs, downs]
    meet(rings)

    def stage():
        for ring in rings:
            if ring.left():
                ring.step()

    stage()
    dmid, dr_own, gain_fi, gain_ao = small_call(
        functools.partial(turn_kernel, len(shares)),
        [struct((size, width), F32), block, vector, vector],
        (*together(shares, bigs.blocks[0]), middle, cotangent, branch, g_fi, g_ao),
    )
    meet(rings, dr_own, output)

    dr_all = flat(gather_rows(dr_own))
    dr_used = [dr_all[i] for i in q_blocks]
    stage()
    grads, gain_q, gain_k, *da_parts = small_call(
        functools.partial(attend_back_kernel, q_count, q_blocks, group),
        [struct((rows, 3 * HD), BF16), struct((1, HD), F32), struct((1, HD), F32)] + [block] * group,
        (
            *dr_used,
            *(prob, raw, query, key, value, qkv_full, out_full, cosine, sine, g_q, g_k),
        ),
        scratch=[pltpu.VMEM((rows, HD), F32)] * 2,
    )
    meet(rings, grads)
    shares, sent = scatter_rows(by_tensor(da_parts))
    stage()
    smalls = RingSum(outer([(a_all, [grads]), (dr_used, [o])], spot_line))
    rings.append(smalls)
    meet(rings, *sent)
    stage()
    input_grad, gain_in = small_call(
        functools.partial(last_kernel, len(shares)),
        [block, vector],
        (*shares, x, dmid, g_in),
    )
    gain_grads = (gain_in, gain_ao, gain_fi, gain_fo, gain_q, gain_k)
    packed = jnp.concatenate([g.reshape(seqs * cores, -1) for g in gain_grads], axis=1)
    meet(rings, input_grad, packed)
    input_grad = from_rows(input_grad)
    near = [e for e in exchanges() if e[0] != "seq"]
    far = [e for e in exchanges() if e[0] == "seq"]
    for way in near:
        packed = exchange(packed, *way)
    stage()
    meet(rings, packed)
    while bigs.left():
        stage()
        meet(rings, input_grad)
    (packed,) = together([packed], bigs.sum)
    while smalls.left() or far:
        if smalls.left():
            smalls.step()
        if far:
            packed = exchange(packed, *far.pop(0))
            smalls.wait(packed)
            (packed,) = together([packed], smalls.sum)
    down_sum, small_sum = downs.sum, smalls.sum
    gate_sum, up_sum = bigs.sum[:, :hidden], bigs.sum[:, hidden:]

    def to_owner(values):
        values = values.astype(F32)
        if cores != 2:
            return lax.all_to_all(values, "core", split_axis=0, concat_axis=1, tiled=True)
        halves = values.reshape(cores, own_feats, -1)
        mine = pick(halves, c_index, 0)
        other = shift(pick(halves, 1 - c_index, 0), "core", 1)
        return jnp.where(
            c_index == 0, jnp.concatenate([mine, other], axis=1), jnp.concatenate([other, mine], axis=1)
        )

    def sum_core(values):
        values = values.astype(F32)
        if cores != 2:
            return lax.psum_scatter(values, "core", scatter_dimension=0, tiled=True)
        halves = values.reshape(cores, own_feats, -1)
        return pick(halves, c_index, 0) + shift(pick(halves, 1 - c_index, 0), "core", 1)

    kv_sum = sum_tensor(sum_core(small_sum[:, HD : 3 * HD]))
    own_columns = to_owner if split_heads else sum_core
    q_grad, out_grad_w = own_columns(small_sum[:, :HD]), own_columns(small_sum[:, 3 * HD :])
    mine = pick(packed, s_index * cores + c_index, 0)
    gain_out = tuple(mine[end - n : end] for end, n in zip(gain_ends, gain_sizes))
    return (
        output,
        input_grad,
        q_grad,
        kv_sum[:, :HD],
        kv_sum[:, HD:],
        out_grad_w,
        to_owner(gate_sum[:, :hidden_here]),
        to_owner(up_sum[:, :hidden_here]),
        to_owner(down_sum[:, :hidden_here]),
    ) + gain_out


def solution(mesh):
    def run(tokens, *rest):
        seqs = tokens.shape[0] * tokens.shape[1]
        wide, tensor = mesh.shape["wide"], mesh.shape["tensor"]
        fine = Mesh(mesh.devices.reshape(seqs, wide // seqs, tensor), ("seq", "core", "tensor"))
        acts = P(None, None, ("seq", "core", "tensor"), None)
        both = P(("seq", "core"), "tensor")
        rows = P(("seq", "core"), None)
        vector = P(("seq", "core"))
        weights = (both, rows, rows, both, both, both, both) + (vector,) * 6
        return jax.shard_map(
            body,
            mesh=fine,
            in_specs=(acts, acts, P(), P()) + weights,
            out_specs=(acts, acts) + weights,
            check_vma=False,
        )(tokens, *rest)

    return run
```

```python
import functools

import jax
import jax.numpy as jnp
from jax import lax
from jax.experimental import pallas as pl
from jax.experimental.pallas import tpu as pltpu
from jax.sharding import Mesh
from jax.sharding import PartitionSpec as P

HD = 256
PIC = 256
EPSILON = 1e-06
ROPE_BASE = 1000000.0
SCALE = HD ** (-0.5)
TILE = 256
F32 = jnp.float32
BF16 = jnp.bfloat16


def dot(left, right, dims):
    return lax.dot_general(left, right, ((dims[0], dims[1]), ((), ())), preferred_element_type=F32)


def mm(left, right):
    return dot(left, right, ((1,), (0,)))


def mm_nt(left, right):
    return dot(left, right, ((1,), (1,)))


def mm_tn(left, right):
    return dot(left, right, ((0,), (0,)))


def inverse_root(values):
    return lax.rsqrt(jnp.mean(values * values, axis=-1, keepdims=True) + EPSILON)


def norm_back(values, factor, grad):
    root = inverse_root(values)
    scaled = grad * factor
    inner = jnp.mean(values * scaled, axis=-1, keepdims=True)
    grad_values = root * (scaled - values * (root * root * inner))
    return grad_values, jnp.sum(grad * (values * root), axis=0, keepdims=True)


def turn(values, cosine, sine):
    half = values.shape[-1] // 2
    first = values[..., :half]
    second = values[..., half:]
    return jnp.concatenate([first * cosine - second * sine, second * cosine + first * sine], axis=-1)


def gelu_parts(v):
    c = (2.0 / jnp.pi) ** 0.5
    square = v * v
    t = jnp.tanh(c * v * (1.0 + 0.044715 * square))
    value = 0.5 * v * (1.0 + t)
    slope = 0.5 * (1.0 + t) + 0.5 * v * (1.0 - t * t) * (c * (1.0 + 0.134145 * square))
    return value, slope


def call(kernel, outs, ins, scratch=(), mib=48, flops=0, moved=0, **more):
    return pl.pallas_call(
        kernel,
        out_shape=outs,
        scratch_shapes=list(scratch),
        compiler_params=pltpu.CompilerParams(vmem_limit_bytes=mib << 20),
        cost_estimate=pl.CostEstimate(flops=0, bytes_accessed=1, transcendentals=0),
        **more,
    )(*ins)


def small_call(kernel, outs, ins, **more):
    vmem = pl.BlockSpec(memory_space=pltpu.VMEM)
    moved = sum(v.size * v.dtype.itemsize for v in (*ins, *outs))
    return call(
        kernel, outs, ins, in_specs=[vmem] * len(ins), out_specs=[vmem] * len(outs), moved=moved, **more
    )


def struct(shape, kind):
    return jax.ShapeDtypeStruct(shape, kind)


def total_of(refs):
    total = refs[0][...].astype(F32)
    for ref in refs[1:]:
        total = total + ref[...].astype(F32)
    return total


def start_kernel(x_ref, gain_ref, a_ref):
    x = x_ref[...].astype(F32)
    a_ref[...] = (x * inverse_root(x) * gain_ref[...]).astype(BF16)


def middle_kernel(count, *refs):
    x_ref, g_ao, g_fi = refs[count : count + 3]
    r_ref, mid_ref, f_ref = refs[count + 3 :]
    r = total_of(refs[:count])
    mid = x_ref[...].astype(F32) + r * inverse_root(r) * g_ao[...]
    r_ref[...] = r
    mid_ref[...] = mid
    f_ref[...] = (mid * inverse_root(mid) * g_fi[...]).astype(BF16)


def close_kernel(count, *refs):
    mid_ref, cot_ref, g_fo = refs[count : count + 3]
    out_ref, de_ref, gain_ref = refs[count + 3 :]
    e = total_of(refs[:count])
    cot = cot_ref[...].astype(F32)
    out_ref[...] = (mid_ref[...] + e * inverse_root(e) * g_fo[...]).astype(BF16)
    de, gain = norm_back(e, g_fo[...], cot)
    de_ref[...] = de.astype(BF16)
    gain_ref[...] = gain


def turn_kernel(count, *refs):
    mid_ref, cot_ref, r_ref, g_fi, g_ao = refs[count : count + 5]
    dmid_ref, dr_ref, gain_fi, gain_ao = refs[count + 5 :]
    back, gain = norm_back(mid_ref[...], g_fi[...], total_of(refs[:count]))
    gain_fi[...] = gain
    dmid = cot_ref[...].astype(F32) + back
    dmid_ref[...] = dmid
    dr, gain = norm_back(r_ref[...], g_ao[...], dmid)
    gain_ao[...] = gain
    dr_ref[...] = dr.astype(BF16)


def last_kernel(count, *refs):
    x_ref, dmid_ref, g_in = refs[count : count + 3]
    dx_ref, gain_ref = refs[count + 3 :]
    back, gain = norm_back(x_ref[...].astype(F32), g_in[...], total_of(refs[:count]))
    dx_ref[...] = (dmid_ref[...] + back).astype(BF16)
    gain_ref[...] = gain


def attend_kernel(count, q_blocks, *refs):
    a_refs = refs[:count]
    qkv, out_w, cosine, sine, g_q, g_k, meta_q, meta_k = refs[count : count + 8]
    o_ref, prob_ref, raw_ref, q_ref, k_ref, v_ref = refs[count + 8 : count + 14]
    r_refs = refs[count + 14 :]
    size = a_refs[0].shape[0]
    for i, a_ref in enumerate(a_refs):
        rows = slice(i * size, (i + 1) * size)
        raw = mm(a_ref[...], qkv[...])
        raw_ref[rows] = raw[:, : 2 * HD].astype(BF16)
        cos, sin = cosine[rows], sine[rows]
        query, key = raw[:, :HD], raw[:, HD : 2 * HD]
        q_ref[rows] = (turn(query * inverse_root(query) * g_q[...], cos, sin) * SCALE).astype(BF16)
        k_ref[rows] = turn(key * inverse_root(key) * g_k[...], cos, sin).astype(BF16)
        v_ref[rows] = raw[:, 2 * HD :].astype(BF16)
    key_doc, key_place, key_pic = meta_k[0:1], meta_k[1:2], meta_k[2:3]
    for n, i in enumerate(q_blocks):
        rows = slice(i * size, (i + 1) * size)
        done = slice(n * size, (n + 1) * size)
        scores = mm_nt(q_ref[rows], k_ref[...])
        doc, place, pic = meta_q[rows, 0:1], meta_q[rows, 1:2], meta_q[rows, 2:3]
        allowed = (doc == key_doc) & ((key_place <= place) | ((pic == key_pic) & (pic >= 0)))
        scores = jnp.where(allowed, scores, -1e30)
        weight = jnp.exp(scores - jnp.max(scores, axis=-1, keepdims=True))
        prob = (weight * (1.0 / jnp.sum(weight, axis=-1, keepdims=True))).astype(BF16)
        prob_ref[done] = prob
        o = mm(prob, v_ref[...]).astype(BF16)
        o_ref[done] = o
        r_refs[n][...] = mm_nt(o, out_w[...]).astype(BF16)


def attend_back_kernel(count, q_blocks, total, *refs):
    dr_refs = refs[:count]
    prob_ref, raw_ref, q_ref, k_ref, v_ref, qkv, out_w, cosine, sine, g_q, g_k = refs[count : count + 11]
    grad_ref, gain_q, gain_k = refs[count + 11 : count + 14]
    da_refs = refs[count + 14 : count + 14 + total]
    dk_ref, dv_ref = refs[count + 14 + total :]
    size = dr_refs[0].shape[0]
    if len(q_blocks) != total:
        grad_ref[:, :HD] = jnp.zeros((size * total, HD), BF16)
    sum_q = jnp.zeros((1, HD), F32)
    sum_k = jnp.zeros((1, HD), F32)
    for n, i in enumerate(q_blocks):
        rows = slice(i * size, (i + 1) * size)
        done = slice(n * size, (n + 1) * size)
        do = mm(dr_refs[n][...], out_w[...]).astype(BF16)
        prob_low = prob_ref[done]
        prob = prob_low.astype(F32)
        dprob = mm_nt(do, v_ref[...])
        ds = (prob * (dprob - jnp.sum(prob * dprob, axis=-1, keepdims=True))).astype(BF16)
        dq = mm(ds, k_ref[...])
        dk = mm_tn(ds, q_ref[rows])
        dv = mm_tn(prob_low, do)
        if n == 0:
            dk_ref[...] = dk
            dv_ref[...] = dv
        else:
            dk_ref[...] += dk
            dv_ref[...] += dv
        raw = raw_ref[rows, :HD].astype(F32)
        back, gain = norm_back(raw, g_q[...], turn(dq * SCALE, cosine[rows], -sine[rows]))
        grad_ref[rows, :HD] = back.astype(BF16)
        sum_q = sum_q + gain
    for i in range(total):
        rows = slice(i * size, (i + 1) * size)
        raw = raw_ref[rows, HD:].astype(F32)
        back, gain = norm_back(raw, g_k[...], turn(dk_ref[rows], cosine[rows], -sine[rows]))
        grad_ref[rows, HD : 2 * HD] = back.astype(BF16)
        grad_ref[rows, 2 * HD :] = dv_ref[rows].astype(BF16)
        sum_k = sum_k + gain
        da_refs[i][...] = mm_nt(grad_ref[rows], qkv[...]).astype(BF16)
    gain_q[...] = sum_q
    gain_k[...] = sum_k


def hidden_kernel(count, *refs):
    gate_w, up_w, keep_gate, keep_up, hid_ref = refs[count:]
    size = refs[0].shape[0]
    for i in range(count):
        rows = slice(i * size, (i + 1) * size)
        gate = mm(refs[i][...], gate_w[...])
        up = mm(refs[i][...], up_w[...])
        value, slope = gelu_parts(gate)
        keep_gate[rows] = (up * slope).astype(BF16)
        keep_up[rows] = value.astype(BF16)
        hid_ref[rows] = (value * up).astype(BF16)


def down_kernel(hid_ref, down_w, *outs):
    size = outs[0].shape[0]
    part = mm_nt(hid_ref[...], down_w[...]).astype(BF16)
    for i, out in enumerate(outs):
        out[...] = part[i * size : (i + 1) * size]


def hidden_back_kernel(count, *refs):
    keep_gate, keep_up, gate_w, up_w, down_w, dgate_ref, dup_ref = refs[count : count + 7]
    df_refs = refs[count + 7 :]
    size = refs[0].shape[0]
    for i in range(count):
        rows = slice(i * size, (i + 1) * size)
        dhid = mm(refs[i][...], down_w[...])
        dgate_ref[rows] = (dhid * keep_gate[rows].astype(F32)).astype(BF16)
        dup_ref[rows] = (dhid * keep_up[rows].astype(F32)).astype(BF16)
        df_refs[i][...] = (mm_nt(dgate_ref[rows], gate_w[...]) + mm_nt(dup_ref[rows], up_w[...])).astype(BF16)


def hidden_forward(pieces, gate_w, up_w):
    size, hidden = pieces[0].shape[0], gate_w.shape[1]
    return small_call(
        functools.partial(hidden_kernel, len(pieces)),
        [struct((len(pieces) * size, hidden), BF16)] * 3,
        (*pieces, gate_w, up_w),
        mib=24,
    )


def down_forward(hid, down_w, count):
    shape = hid.shape[0] // count, down_w.shape[0]
    return small_call(down_kernel, [struct(shape, BF16)] * count, (hid, down_w), mib=24)


def hidden_backward(pieces, keep_gate, keep_up, gate_w, up_w, down_w):
    size, width = pieces[0].shape
    count, hidden = len(pieces), gate_w.shape[1]
    return small_call(
        functools.partial(hidden_back_kernel, count),
        [struct((count * size, hidden), BF16)] * 2 + [struct((size, width), BF16)] * count,
        (*pieces, keep_gate, keep_up, gate_w, up_w, down_w),
        mib=24,
    )


def outer_kernel(groups, spots, *refs):
    count = spots.shape[0]
    outs, whole, sems = refs[-2 - count : -2], refs[-2], refs[-1]
    feats = whole.shape[0] // count
    used, column, copies = 0, 0, []
    for n, (lefts, rights) in enumerate(groups):
        left = jnp.concatenate([r[...] for r in refs[used : used + lefts]], axis=0)
        right = jnp.concatenate([r[...] for r in refs[used + lefts : used + lefts + rights]], axis=0)
        columns = slice(column, column + right.shape[1])
        whole[:, columns] = mm_tn(left, right).astype(BF16)
        for k, out in enumerate(outs):
            first = pl.multiple_of(spots[(k + 1) % count] * feats, 16)
            copies.append(
                pltpu.make_async_copy(whole.at[pl.ds(first, feats), columns], out.at[:, columns], sems.at[n, k])
            )
            copies[-1].start()
        used, column = used + lefts + rights, columns.stop
    for copy in copies:
        copy.wait()


def outer(products, spots):
    count = spots.shape[0]
    width = products[0][0][0].shape[1]
    total = sum(right[0].shape[1] for _, right in products)
    ins = [v for left, right in products for v in (*left, *right)]
    vmem = pl.BlockSpec(memory_space=pltpu.VMEM)
    return call(
        functools.partial(outer_kernel, [(len(left), len(right)) for left, right in products]),
        [struct((width // count, total), BF16)] * count,
        (spots, *ins),
        scratch=[pltpu.VMEM((width, total), BF16), pltpu.SemaphoreType.DMA((len(products), count))],
        in_specs=[pl.BlockSpec(memory_space=pltpu.SMEM)] + [vmem] * len(ins),
        out_specs=[pl.BlockSpec(memory_space=pl.ANY)] * count,
        mib=32,
    )


def layout(lengths, starts, places):
    doc_ends = jnp.cumsum(lengths)
    before = places[:, None] >= doc_ends[None, :]
    doc_ids = jnp.sum(before.astype(jnp.int32), axis=1)
    opening = jnp.max(jnp.where(before, doc_ends[None, :], 0), axis=1)
    inside = (places[:, None] >= starts[None, :]) & (places[:, None] < starts[None, :] + PIC)
    labels = jnp.arange(1, starts.shape[0] + 1, dtype=jnp.int32)
    pictures = jnp.sum(jnp.where(inside, labels[None, :], 0), axis=1) - 1
    return doc_ids, places - opening, pictures


def shift(values, axis, step):
    size = lax.axis_size(axis)
    return lax.ppermute(values, axis, [(i, (i + step) % size) for i in range(size)])


def gather_rows(own):
    across = [own] + [shift(own, "tensor", k) for k in range(1, lax.axis_size("tensor"))]
    return [[p] + [shift(p, "core", k) for k in range(1, lax.axis_size("core"))] for p in across]


def scatter_rows(parts):
    result, sent = [], []
    for k in list(range(1, len(parts))) + [0]:
        first = [parts[k][0]] + [shift(p, "core", -j) for j, p in enumerate(parts[k]) if j]
        if k:
            total = first[0].astype(F32)
            for p in first[1:]:
                total = total + p.astype(F32)
            sent.append(total.astype(BF16))
            result.append(shift(sent[-1], "tensor", -k))
        else:
            result.extend(first)
    return result, sent


def ring_order(count):
    return list(range(0, count, 2)) + list(range(1, count, 2))[::-1]


def ring_spots():
    count = lax.axis_size("seq")
    ring = ring_order(count)
    table = [
        [[ring[(ring.index(i) - way * k) % count] for k in range(count)] for i in range(count)] for way in (1, -1)
    ]
    line = jnp.array(table, jnp.int32).reshape(2 * count, count)
    row = (lax.axis_index("core") % 2) * count + lax.axis_index("seq")
    line = lax.dynamic_index_in_dim(line, row, 0, keepdims=False, allow_negative_indices=False)
    return line, [line[k] for k in range(count)]


def together(values, *others):
    return lax.optimization_barrier((tuple(values), others))[0]


def hop(values):
    count, cores = lax.axis_size("seq"), lax.axis_size("core")
    ring = ring_order(count)
    pairs = [
        (ring[i] * cores + c, ring[(i + (-1) ** (c % 2)) % count] * cores + c)
        for i in range(count)
        for c in range(cores)
    ]
    return lax.ppermute(values, ("seq", "core"), pairs)


def put(full, block, row, spot):
    return lax.dynamic_update_slice(full, block[None], (spot, row, 0), allow_negative_indices=False)


def pick(array, spot, axis):
    return lax.dynamic_index_in_dim(array, spot, axis, keepdims=False, allow_negative_indices=False)


class RingSum:
    def __init__(self, blocks):
        self.blocks, self.hops = blocks, 0
        self.sum = blocks[0]

    def left(self):
        return len(self.blocks) - 1 - self.hops

    def step(self):
        self.hops += 1
        total = hop(self.sum).astype(F32) + self.blocks[self.hops].astype(F32)
        self.sum = total if self.left() == 0 else total.astype(BF16)

    def wait(self, *others):
        (self.sum,) = together([self.sum], *others)


def meet(rings, *others):
    values = [ring.sum for ring in rings]
    for ring in rings:
        ring.wait(*values, *others)


def exchanges():
    hops = []
    for axis in ("core", "tensor", "seq"):
        distance = 1
        while distance < lax.axis_size(axis):
            hops.append((axis, distance))
            distance *= 2
    return hops


def exchange(values, axis, distance):
    return values + lax.ppermute(values, axis, [(i, i ^ distance) for i in range(lax.axis_size(axis))])


def sum_tensor(values):
    if lax.axis_size("tensor") == 2:
        return values + shift(values, "tensor", 1)
    return lax.psum(values, "tensor")


def body(
    tokens,
    out_grad,
    doc_lengths,
    picture_starts,
    q_weight,
    k_weight,
    v_weight,
    out_weight,
    gate_weight,
    up_weight,
    down_weight,
    attn_in_gain,
    attn_out_gain,
    ffn_in_gain,
    ffn_out_gain,
    query_gain,
    key_gain,
):
    seqs = lax.axis_size("seq")
    cores = lax.axis_size("core")
    tensors = lax.axis_size("tensor")
    s_index = lax.axis_index("seq")
    c_index = lax.axis_index("core")
    t_index = lax.axis_index("tensor")
    micro, per_micro, span, width = tokens.shape
    split_heads = q_weight.shape[1] > HD
    assert q_weight.shape[1] == HD * (cores if split_heads else 1)
    own_feats = k_weight.shape[0]
    feats = own_feats * cores
    hidden_here = gate_weight.shape[1] // cores
    hidden = -(-hidden_here // TILE) * TILE

    def to_columns(arrays, padded):
        parts = [w.reshape(own_feats, cores, -1).transpose(1, 0, 2) for w in arrays]
        parts = [jnp.pad(p, ((0, 0), (0, 0), (0, padded - p.shape[2]))) for p in parts]
        moved = lax.all_to_all(jnp.concatenate(parts, axis=2), "core", split_axis=0, concat_axis=0, tiled=True)
        moved = moved.reshape(feats, -1)
        return [moved[:, i * padded : (i + 1) * padded] for i in range(len(arrays))]

    def to_rows(*arrays):
        values = jnp.concatenate([v.reshape(seqs, span, width) for v in arrays], axis=1)
        moved = lax.all_to_all(values, "seq", split_axis=0, concat_axis=0, tiled=True)
        return [moved[:, i * span : (i + 1) * span].reshape(seqs * span, width) for i in range(len(arrays))]

    def from_rows(values):
        moved = lax.all_to_all(values.reshape(seqs, span, width), "seq", split_axis=0, concat_axis=0, tiled=True)
        return moved.reshape(micro, per_micro, span, width)

    spot_line, spots = ring_spots()
    gains = (attn_in_gain, attn_out_gain, ffn_in_gain, ffn_out_gain, query_gain, key_gain)
    gain_sizes = [v.shape[0] for v in gains]
    gain_ends = [sum(gain_sizes[: i + 1]) for i in range(6)]
    gain_row = sum(jnp.pad(v, (e - n, 2 * HD - e)) for v, e, n in zip(gains, gain_ends, gain_sizes))
    gain_row = jnp.pad(gain_row[None, :], ((0, -(own_feats + 1) % 16), (0, 0)))
    kv_block = jnp.concatenate([jnp.concatenate([k_weight, v_weight], axis=1), gain_row], axis=0)
    some = jnp.concatenate([q_weight, out_weight], axis=1)
    some = jnp.concatenate([kv_block, jnp.pad(some, ((0, kv_block.shape[0] - own_feats), (0, 0)))], axis=1)
    moving = some
    some = put(jnp.zeros((seqs,) + some.shape, BF16), some, 0, spots[0])
    gain_rows = moving[own_feats:, : 2 * HD]
    gain_rows = put(jnp.zeros((seqs,) + gain_rows.shape, BF16), gain_rows, 0, spots[0])
    (x,) = to_rows(tokens)
    for step in range(1, seqs):
        if step == 5:
            moving = together([moving], x)[0]
        moving = hop(moving)
        some = put(some, moving, 0, spots[step])
        gain_rows = put(gain_rows, moving[own_feats:, : 2 * HD], 0, spots[step])
    early = moving
    def with_core(values):
        if cores != 2:
            return lax.all_gather(values, "core", axis=1)
        other = shift(values, "core", 1)
        return jnp.where(c_index == 0, jnp.stack([values, other], axis=1), jnp.stack([other, values], axis=1))

    gain_all = with_core(gain_rows)[:, :, 0].astype(F32)
    some = with_core(some)
    some = some.reshape((seqs * cores,) + some.shape[2:])
    first = 2 * HD + (c_index * HD if split_heads else 0)

    def columns(start, many):
        return lax.dynamic_slice(
            some, (0, 0, start), (seqs * cores, own_feats, many), allow_negative_indices=False
        ).reshape(width, many)

    q_full = columns(first, HD)
    out_full = columns(first + q_weight.shape[1], HD)
    qkv_full = jnp.concatenate([q_full, columns(0, 2 * HD)], axis=1)
    g_in, g_ao, g_fi, g_fo, g_q, g_k = (
        gain_all[:, :, end - size : end].reshape(1, -1) for end, size in zip(gain_ends, gain_sizes)
    )

    size = seqs * span
    group = cores * tensors
    rows = size * group

    owner_tensor = ((t_index - jnp.arange(tensors, dtype=jnp.int32)) % tensors)[:, None, None, None]
    owner_core = ((c_index - jnp.arange(cores, dtype=jnp.int32)) % cores)[None, :, None, None]
    block_index = jnp.arange(seqs, dtype=jnp.int32)[None, None, :, None]
    inner = jnp.arange(span, dtype=jnp.int32)[None, None, None, :]
    places = (((block_index * cores + owner_core) * tensors + owner_tensor) * span + inner).reshape(-1)
    docs, within, pics = layout(
        *(pick(v.reshape(seqs, -1), s_index, 0) for v in (doc_lengths, picture_starts)), places
    )
    frequency = ROPE_BASE ** (-2.0 * jnp.arange(HD // 2, dtype=F32) / HD)
    angles = within.astype(F32)[:, None] * frequency[None, :]
    cosine = jnp.cos(angles)
    sine = jnp.sin(angles)
    meta = [docs, places, pics] + [jnp.zeros_like(docs)] * 5
    meta_q = jnp.stack(meta, axis=1)
    meta_k = jnp.stack(meta, axis=0)
    q_blocks = list(range(group)) if split_heads else [k * cores for k in range(tensors)]
    q_count = len(q_blocks)
    block = struct((size, width), BF16)
    vector = struct((1, width), F32)

    def flat(lists):
        return [p for line in lists for p in line]

    def by_tensor(pieces):
        return [pieces[k * cores : (k + 1) * cores] for k in range(tensors)]

    (a_own,) = small_call(start_kernel, [block], (x, g_in))
    a_all = flat(gather_rows(a_own))
    low_rows = struct((rows, HD), BF16)
    o, prob, raw, query, key, value, *r_parts = small_call(
        functools.partial(attend_kernel, group, q_blocks),
        [struct((q_count * size, HD), BF16), struct((q_count * size, rows), BF16), struct((rows, 2 * HD), BF16)]
        + [low_rows] * 3
        + [block] * q_count,
        (*a_all, qkv_full, out_full, cosine, sine, g_q, g_k, meta_q, meta_k),
        flops=2 * rows * width * 3 * HD + 2 * q_count * size * HD * (2 * rows + width),
    )
    if q_count != group:
        spread = [jnp.zeros((size, width), BF16)] * group
        for i, part in zip(q_blocks, r_parts):
            spread[i] = part
        r_parts = spread
    shares, sent = scatter_rows(by_tensor(r_parts))

    branch, middle, f_own = small_call(
        functools.partial(middle_kernel, len(shares)),
        [struct((size, width), F32)] * 2 + [block],
        (*shares, x, g_ao, g_fi),
    )
    f_all = gather_rows(f_own)

    blocks = to_columns([gate_weight, up_weight, down_weight], hidden)
    moving = together(blocks, early)
    fulls = [put(jnp.zeros((seqs, feats, hidden), BF16), v, 0, spots[0]) for v in moving]
    ahead = {2: (0, [a_own]), 3: (1, [qkv_full, out_full]), 4: (2, sent), 6: (0, [f_own])}
    for step in range(1, seqs):
        if step in ahead:
            chain, values = ahead[step]
            moving = list(moving)
            (moving[chain],) = together([moving[chain]], *values)
        moving = [hop(v) for v in moving]
        if step == seqs - 2:
            nearly = moving
        fulls = [put(full, v, 0, spots[step]) for full, v in zip(fulls, moving)]
    gate_full, up_full, down_full = fulls
    gate_full, up_full, down_full = (w.reshape(width, hidden) for w in (gate_full, up_full, down_full))
    f_pieces = flat(f_all)
    keep_gate, keep_up, hid = hidden_forward(f_pieces, gate_full, up_full)
    (cotangent,) = to_rows(*together([out_grad], *nearly))
    shares, _ = scatter_rows(by_tensor(down_forward(hid, down_full, group)))
    output, de_own, gain_fo = small_call(
        functools.partial(close_kernel, len(shares)),
        [block, block, vector],
        (*shares, middle, cotangent, g_fo),
    )

    output = from_rows(output)
    de_all = flat(gather_rows(de_own))
    downs = RingSum(outer([(de_all, together([hid], output))], spot_line))
    dgate, dup, *df_parts = hidden_backward(
        together(de_all, downs.sum), keep_gate, keep_up, gate_full, up_full, down_full
    )
    downs.step()
    downs.wait(dgate)
    shares, _ = scatter_rows(by_tensor(df_parts))
    gates = RingSum(outer([(f_pieces, together([dgate], downs.sum))], spot_line))
    downs.step()
    downs.wait(gates.sum)
    first_gate = gates.sum
    gates.step()
    ups = RingSum(outer([(f_pieces, together([dup], first_gate, downs.sum))], spot_line))
    downs.step()
    rings = [ups, gates, downs]
    meet(rings)

    def stage():
        for ring in rings:
            if ring.left():
                ring.step()

    stage()
    dmid, dr_own, gain_fi, gain_ao = small_call(
        functools.partial(turn_kernel, len(shares)),
        [struct((size, width), F32), block, vector, vector],
        (*together(shares, ups.blocks[0]), middle, cotangent, branch, g_fi, g_ao),
    )
    meet(rings, dr_own)

    dr_all = flat(gather_rows(dr_own))
    dr_used = [dr_all[i] for i in q_blocks]
    stage()
    grads, gain_q, gain_k, *da_parts = small_call(
        functools.partial(attend_back_kernel, q_count, q_blocks, group),
        [struct((rows, 3 * HD), BF16), struct((1, HD), F32), struct((1, HD), F32)] + [block] * group,
        (
            *dr_used,
            *(prob, raw, query, key, value, qkv_full, out_full, cosine, sine, g_q, g_k),
        ),
        scratch=[pltpu.VMEM((rows, HD), F32)] * 2,
    )
    meet(rings, grads)
    shares, sent = scatter_rows(by_tensor(da_parts))
    stage()
    smalls = RingSum(outer([(a_all, [grads]), (dr_used, [o])], spot_line))
    smalls.step()
    meet(rings, *sent)
    smalls.wait(ups.sum)
    smalls.step()
    stage()
    input_grad, gain_in = small_call(
        functools.partial(last_kernel, len(shares)),
        [block, vector],
        (*shares, x, dmid, g_in),
    )
    gain_grads = (gain_in, gain_ao, gain_fi, gain_fo, gain_q, gain_k)
    packed = jnp.concatenate([g.reshape(seqs * cores, -1) for g in gain_grads], axis=1)
    rings.append(smalls)
    meet(rings, input_grad, packed)
    input_grad = from_rows(input_grad)
    for way in [e for e in exchanges() if e[0] != "seq"]:
        packed = exchange(packed, *way)
    far = [e for e in exchanges() if e[0] == "seq"]
    while ups.left():
        stage()
        meet(rings, packed)
    (packed,) = together([packed], ups.sum)
    while smalls.left() or far:
        if smalls.left():
            smalls.step()
        if far:
            packed = exchange(packed, *far.pop(0))
        smalls.wait(packed)
        (packed,) = together([packed], smalls.sum)
    down_sum, small_sum = downs.sum, smalls.sum
    gate_sum, up_sum = gates.sum, ups.sum

    def to_owner(values):
        values = values.astype(F32)
        if cores != 2:
            return lax.all_to_all(values, "core", split_axis=0, concat_axis=1, tiled=True)
        halves = values.reshape(cores, own_feats, -1)
        mine = pick(halves, c_index, 0)
        other = shift(pick(halves, 1 - c_index, 0), "core", 1)
        return jnp.where(
            c_index == 0, jnp.concatenate([mine, other], axis=1), jnp.concatenate([other, mine], axis=1)
        )

    def sum_core(values):
        values = values.astype(F32)
        if cores != 2:
            return lax.psum_scatter(values, "core", scatter_dimension=0, tiled=True)
        halves = values.reshape(cores, own_feats, -1)
        return pick(halves, c_index, 0) + shift(pick(halves, 1 - c_index, 0), "core", 1)

    kv_sum = sum_tensor(sum_core(small_sum[:, HD : 3 * HD]))
    own_columns = to_owner if split_heads else sum_core
    q_grad, out_grad_w = own_columns(small_sum[:, :HD]), own_columns(small_sum[:, 3 * HD :])
    mine = pick(packed, s_index * cores + c_index, 0)
    gain_out = tuple(mine[end - n : end] for end, n in zip(gain_ends, gain_sizes))
    return (
        output,
        input_grad,
        q_grad,
        kv_sum[:, :HD],
        kv_sum[:, HD:],
        out_grad_w,
        to_owner(gate_sum[:, :hidden_here]),
        to_owner(up_sum[:, :hidden_here]),
        to_owner(down_sum[:, :hidden_here]),
    ) + gain_out


def solution(mesh):
    def run(tokens, *rest):
        seqs = tokens.shape[0] * tokens.shape[1]
        wide, tensor = mesh.shape["wide"], mesh.shape["tensor"]
        fine = Mesh(mesh.devices.reshape(seqs, wide // seqs, tensor), ("seq", "core", "tensor"))
        acts = P(None, None, ("seq", "core", "tensor"), None)
        both = P(("seq", "core"), "tensor")
        rows = P(("seq", "core"), None)
        vector = P(("seq", "core"))
        weights = (both, rows, rows, both, both, both, both) + (vector,) * 6
        return jax.shard_map(
            body,
            mesh=fine,
            in_specs=(acts, acts, P(), P()) + weights,
            out_specs=(acts, acts) + weights,
            check_vma=False,
        )(tokens, *rest)

    return run
```

```python
import functools

import jax
import jax.numpy as jnp
from jax import lax
from jax.experimental import pallas as pl
from jax.experimental.pallas import tpu as pltpu
from jax.sharding import Mesh
from jax.sharding import PartitionSpec as P

HD = 256
PIC = 256
EPSILON = 1e-06
ROPE_BASE = 1000000.0
SCALE = HD ** (-0.5)
TILE = 256
F32 = jnp.float32
BF16 = jnp.bfloat16


def dot(left, right, dims):
    return lax.dot_general(left, right, ((dims[0], dims[1]), ((), ())), preferred_element_type=F32)


def mm(left, right):
    return dot(left, right, ((1,), (0,)))


def mm_nt(left, right):
    return dot(left, right, ((1,), (1,)))


def mm_tn(left, right):
    return dot(left, right, ((0,), (0,)))


def inverse_root(values):
    return lax.rsqrt(jnp.mean(values * values, axis=-1, keepdims=True) + EPSILON)


def norm_back(values, factor, grad):
    root = inverse_root(values)
    scaled = grad * factor
    inner = jnp.mean(values * scaled, axis=-1, keepdims=True)
    grad_values = root * (scaled - values * (root * root * inner))
    return grad_values, jnp.sum(grad * (values * root), axis=0, keepdims=True)


def turn(values, cosine, sine):
    half = values.shape[-1] // 2
    first = values[..., :half]
    second = values[..., half:]
    return jnp.concatenate([first * cosine - second * sine, second * cosine + first * sine], axis=-1)


def gelu_parts(v):
    c = (2.0 / jnp.pi) ** 0.5
    square = v * v
    t = jnp.tanh(c * v * (1.0 + 0.044715 * square))
    value = 0.5 * v * (1.0 + t)
    slope = 0.5 * (1.0 + t) + 0.5 * v * (1.0 - t * t) * (c * (1.0 + 0.134145 * square))
    return value, slope


def call(kernel, outs, ins, scratch=(), mib=48, flops=0, moved=0, **more):
    return pl.pallas_call(
        kernel,
        out_shape=outs,
        scratch_shapes=list(scratch),
        compiler_params=pltpu.CompilerParams(vmem_limit_bytes=mib << 20),
        cost_estimate=pl.CostEstimate(flops=0, bytes_accessed=1, transcendentals=0),
        **more,
    )(*ins)


def small_call(kernel, outs, ins, **more):
    vmem = pl.BlockSpec(memory_space=pltpu.VMEM)
    moved = sum(v.size * v.dtype.itemsize for v in (*ins, *outs))
    return call(
        kernel, outs, ins, in_specs=[vmem] * len(ins), out_specs=[vmem] * len(outs), moved=moved, **more
    )


def struct(shape, kind):
    return jax.ShapeDtypeStruct(shape, kind)


def total_of(refs):
    total = refs[0][...].astype(F32)
    for ref in refs[1:]:
        total = total + ref[...].astype(F32)
    return total


def start_kernel(x_ref, gain_ref, a_ref):
    x = x_ref[...].astype(F32)
    a_ref[...] = (x * inverse_root(x) * gain_ref[...]).astype(BF16)


def middle_kernel(count, *refs):
    x_ref, g_ao, g_fi = refs[count : count + 3]
    r_ref, mid_ref, f_ref = refs[count + 3 :]
    r = total_of(refs[:count])
    mid = x_ref[...].astype(F32) + r * inverse_root(r) * g_ao[...]
    r_ref[...] = r
    mid_ref[...] = mid
    f_ref[...] = (mid * inverse_root(mid) * g_fi[...]).astype(BF16)


def close_kernel(count, *refs):
    mid_ref, cot_ref, g_fo = refs[count : count + 3]
    out_ref, de_ref, gain_ref = refs[count + 3 :]
    e = total_of(refs[:count])
    cot = cot_ref[...].astype(F32)
    out_ref[...] = (mid_ref[...] + e * inverse_root(e) * g_fo[...]).astype(BF16)
    de, gain = norm_back(e, g_fo[...], cot)
    de_ref[...] = de.astype(BF16)
    gain_ref[...] = gain


def turn_kernel(count, *refs):
    mid_ref, cot_ref, r_ref, g_fi, g_ao = refs[count : count + 5]
    dmid_ref, dr_ref, gain_fi, gain_ao = refs[count + 5 :]
    back, gain = norm_back(mid_ref[...], g_fi[...], total_of(refs[:count]))
    gain_fi[...] = gain
    dmid = cot_ref[...].astype(F32) + back
    dmid_ref[...] = dmid
    dr, gain = norm_back(r_ref[...], g_ao[...], dmid)
    gain_ao[...] = gain
    dr_ref[...] = dr.astype(BF16)


def last_kernel(count, *refs):
    x_ref, dmid_ref, g_in = refs[count : count + 3]
    dx_ref, gain_ref = refs[count + 3 :]
    back, gain = norm_back(x_ref[...].astype(F32), g_in[...], total_of(refs[:count]))
    dx_ref[...] = (dmid_ref[...] + back).astype(BF16)
    gain_ref[...] = gain


def attend_kernel(count, q_blocks, *refs):
    a_refs = refs[:count]
    qkv, out_w, cosine, sine, g_q, g_k, meta_q, meta_k = refs[count : count + 8]
    o_ref, prob_ref, raw_ref, q_ref, k_ref, v_ref = refs[count + 8 : count + 14]
    r_refs = refs[count + 14 :]
    size = a_refs[0].shape[0]
    for i, a_ref in enumerate(a_refs):
        rows = slice(i * size, (i + 1) * size)
        raw = mm(a_ref[...], qkv[...])
        raw_ref[rows] = raw[:, : 2 * HD].astype(BF16)
        cos, sin = cosine[rows], sine[rows]
        query, key = raw[:, :HD], raw[:, HD : 2 * HD]
        q_ref[rows] = (turn(query * inverse_root(query) * g_q[...], cos, sin) * SCALE).astype(BF16)
        k_ref[rows] = turn(key * inverse_root(key) * g_k[...], cos, sin).astype(BF16)
        v_ref[rows] = raw[:, 2 * HD :].astype(BF16)
    key_doc, key_place, key_pic = meta_k[0:1], meta_k[1:2], meta_k[2:3]
    for n, i in enumerate(q_blocks):
        rows = slice(i * size, (i + 1) * size)
        done = slice(n * size, (n + 1) * size)
        scores = mm_nt(q_ref[rows], k_ref[...])
        doc, place, pic = meta_q[rows, 0:1], meta_q[rows, 1:2], meta_q[rows, 2:3]
        allowed = (doc == key_doc) & ((key_place <= place) | ((pic == key_pic) & (pic >= 0)))
        scores = jnp.where(allowed, scores, -1e30)
        weight = jnp.exp(scores - jnp.max(scores, axis=-1, keepdims=True))
        prob = (weight * (1.0 / jnp.sum(weight, axis=-1, keepdims=True))).astype(BF16)
        prob_ref[done] = prob
        o = mm(prob, v_ref[...]).astype(BF16)
        o_ref[done] = o
        r_refs[n][...] = mm_nt(o, out_w[...]).astype(BF16)


def attend_back_kernel(count, q_blocks, total, *refs):
    dr_refs = refs[:count]
    prob_ref, raw_ref, q_ref, k_ref, v_ref, qkv, out_w, cosine, sine, g_q, g_k = refs[count : count + 11]
    grad_ref, gain_q, gain_k = refs[count + 11 : count + 14]
    da_refs = refs[count + 14 : count + 14 + total]
    dk_ref, dv_ref = refs[count + 14 + total :]
    size = dr_refs[0].shape[0]
    if len(q_blocks) != total:
        grad_ref[:, :HD] = jnp.zeros((size * total, HD), BF16)
    sum_q = jnp.zeros((1, HD), F32)
    sum_k = jnp.zeros((1, HD), F32)
    for n, i in enumerate(q_blocks):
        rows = slice(i * size, (i + 1) * size)
        done = slice(n * size, (n + 1) * size)
        do = mm(dr_refs[n][...], out_w[...]).astype(BF16)
        prob_low = prob_ref[done]
        prob = prob_low.astype(F32)
        dprob = mm_nt(do, v_ref[...])
        ds = (prob * (dprob - jnp.sum(prob * dprob, axis=-1, keepdims=True))).astype(BF16)
        dq = mm(ds, k_ref[...])
        dk = mm_tn(ds, q_ref[rows])
        dv = mm_tn(prob_low, do)
        if n == 0:
            dk_ref[...] = dk
            dv_ref[...] = dv
        else:
            dk_ref[...] += dk
            dv_ref[...] += dv
        raw = raw_ref[rows, :HD].astype(F32)
        back, gain = norm_back(raw, g_q[...], turn(dq * SCALE, cosine[rows], -sine[rows]))
        grad_ref[rows, :HD] = back.astype(BF16)
        sum_q = sum_q + gain
    for i in range(total):
        rows = slice(i * size, (i + 1) * size)
        raw = raw_ref[rows, HD:].astype(F32)
        back, gain = norm_back(raw, g_k[...], turn(dk_ref[rows], cosine[rows], -sine[rows]))
        grad_ref[rows, HD : 2 * HD] = back.astype(BF16)
        grad_ref[rows, 2 * HD :] = dv_ref[rows].astype(BF16)
        sum_k = sum_k + gain
        da_refs[i][...] = mm_nt(grad_ref[rows], qkv[...]).astype(BF16)
    gain_q[...] = sum_q
    gain_k[...] = sum_k


def hidden_kernel(count, *refs):
    gate_w, up_w, keep_gate, keep_up, hid_ref = refs[count:]
    size = refs[0].shape[0]
    for i in range(count):
        rows = slice(i * size, (i + 1) * size)
        gate = mm(refs[i][...], gate_w[...])
        up = mm(refs[i][...], up_w[...])
        value, slope = gelu_parts(gate)
        keep_gate[rows] = (up * slope).astype(BF16)
        keep_up[rows] = value.astype(BF16)
        hid_ref[rows] = (value * up).astype(BF16)


def down_kernel(hid_ref, down_w, *outs):
    size = outs[0].shape[0]
    part = mm_nt(hid_ref[...], down_w[...]).astype(BF16)
    for i, out in enumerate(outs):
        out[...] = part[i * size : (i + 1) * size]


def hidden_back_kernel(count, *refs):
    keep_gate, keep_up, gate_w, up_w, down_w, dgate_ref, dup_ref = refs[count : count + 7]
    df_refs = refs[count + 7 :]
    size = refs[0].shape[0]
    for i in range(count):
        rows = slice(i * size, (i + 1) * size)
        dhid = mm(refs[i][...], down_w[...])
        dgate_ref[rows] = (dhid * keep_gate[rows].astype(F32)).astype(BF16)
        dup_ref[rows] = (dhid * keep_up[rows].astype(F32)).astype(BF16)
        df_refs[i][...] = (mm_nt(dgate_ref[rows], gate_w[...]) + mm_nt(dup_ref[rows], up_w[...])).astype(BF16)


def hidden_forward(pieces, gate_w, up_w):
    size, hidden = pieces[0].shape[0], gate_w.shape[1]
    return small_call(
        functools.partial(hidden_kernel, len(pieces)),
        [struct((len(pieces) * size, hidden), BF16)] * 3,
        (*pieces, gate_w, up_w),
        mib=24,
    )


def down_forward(hid, down_w, count):
    shape = hid.shape[0] // count, down_w.shape[0]
    return small_call(down_kernel, [struct(shape, BF16)] * count, (hid, down_w), mib=24)


def hidden_backward(pieces, keep_gate, keep_up, gate_w, up_w, down_w):
    size, width = pieces[0].shape
    count, hidden = len(pieces), gate_w.shape[1]
    return small_call(
        functools.partial(hidden_back_kernel, count),
        [struct((count * size, hidden), BF16)] * 2 + [struct((size, width), BF16)] * count,
        (*pieces, keep_gate, keep_up, gate_w, up_w, down_w),
        mib=24,
    )


def outer_kernel(groups, spots, *refs):
    count = spots.shape[0]
    outs, whole, sems = refs[-2 - count : -2], refs[-2], refs[-1]
    feats = whole.shape[0] // count
    used, column, copies = 0, 0, []
    for n, (lefts, rights) in enumerate(groups):
        left = jnp.concatenate([r[...] for r in refs[used : used + lefts]], axis=0)
        right = jnp.concatenate([r[...] for r in refs[used + lefts : used + lefts + rights]], axis=0)
        columns = slice(column, column + right.shape[1])
        whole[:, columns] = mm_tn(left, right).astype(BF16)
        for k, out in enumerate(outs):
            first = pl.multiple_of(spots[(k + 1) % count] * feats, 16)
            copies.append(
                pltpu.make_async_copy(whole.at[pl.ds(first, feats), columns], out.at[:, columns], sems.at[n, k])
            )
            copies[-1].start()
        used, column = used + lefts + rights, columns.stop
    for copy in copies:
        copy.wait()


def outer(products, spots):
    count = spots.shape[0]
    width = products[0][0][0].shape[1]
    total = sum(right[0].shape[1] for _, right in products)
    ins = [v for left, right in products for v in (*left, *right)]
    vmem = pl.BlockSpec(memory_space=pltpu.VMEM)
    return call(
        functools.partial(outer_kernel, [(len(left), len(right)) for left, right in products]),
        [struct((width // count, total), BF16)] * count,
        (spots, *ins),
        scratch=[pltpu.VMEM((width, total), BF16), pltpu.SemaphoreType.DMA((len(products), count))],
        in_specs=[pl.BlockSpec(memory_space=pltpu.SMEM)] + [vmem] * len(ins),
        out_specs=[pl.BlockSpec(memory_space=pl.ANY)] * count,
        mib=32,
    )


def layout(lengths, starts, places):
    doc_ends = jnp.cumsum(lengths)
    before = places[:, None] >= doc_ends[None, :]
    doc_ids = jnp.sum(before.astype(jnp.int32), axis=1)
    opening = jnp.max(jnp.where(before, doc_ends[None, :], 0), axis=1)
    inside = (places[:, None] >= starts[None, :]) & (places[:, None] < starts[None, :] + PIC)
    labels = jnp.arange(1, starts.shape[0] + 1, dtype=jnp.int32)
    pictures = jnp.sum(jnp.where(inside, labels[None, :], 0), axis=1) - 1
    return doc_ids, places - opening, pictures


def shift(values, axis, step):
    size = lax.axis_size(axis)
    return lax.ppermute(values, axis, [(i, (i + step) % size) for i in range(size)])


def gather_rows(own):
    across = [own] + [shift(own, "tensor", k) for k in range(1, lax.axis_size("tensor"))]
    return [[p] + [shift(p, "core", k) for k in range(1, lax.axis_size("core"))] for p in across]


def scatter_rows(parts):
    result, sent = [], []
    for k in list(range(1, len(parts))) + [0]:
        first = [parts[k][0]] + [shift(p, "core", -j) for j, p in enumerate(parts[k]) if j]
        if k:
            total = first[0].astype(F32)
            for p in first[1:]:
                total = total + p.astype(F32)
            sent.append(total.astype(BF16))
            result.append(shift(sent[-1], "tensor", -k))
        else:
            result.extend(first)
    return result, sent


def ring_order(count):
    return list(range(0, count, 2)) + list(range(1, count, 2))[::-1]


def ring_spots():
    count = lax.axis_size("seq")
    ring = ring_order(count)
    table = [
        [[ring[(ring.index(i) - way * k) % count] for k in range(count)] for i in range(count)] for way in (1, -1)
    ]
    line = jnp.array(table, jnp.int32).reshape(2 * count, count)
    row = (lax.axis_index("core") % 2) * count + lax.axis_index("seq")
    line = lax.dynamic_index_in_dim(line, row, 0, keepdims=False, allow_negative_indices=False)
    return line, [line[k] for k in range(count)]


def together(values, *others):
    return lax.optimization_barrier((tuple(values), others))[0]


def hop(values):
    count, cores = lax.axis_size("seq"), lax.axis_size("core")
    ring = ring_order(count)
    pairs = [
        (ring[i] * cores + c, ring[(i + (-1) ** (c % 2)) % count] * cores + c)
        for i in range(count)
        for c in range(cores)
    ]
    return lax.ppermute(values, ("seq", "core"), pairs)


def put(full, block, row, spot):
    return lax.dynamic_update_slice(full, block[None], (spot, row, 0), allow_negative_indices=False)


def pick(array, spot, axis):
    return lax.dynamic_index_in_dim(array, spot, axis, keepdims=False, allow_negative_indices=False)


class RingSum:
    def __init__(self, blocks):
        self.blocks, self.hops = blocks, 0
        self.sum = self.before = blocks[0]

    def left(self):
        return len(self.blocks) - 1 - self.hops

    def step(self):
        self.hops += 1
        self.before = self.sum
        total = hop(self.sum).astype(F32) + self.blocks[self.hops].astype(F32)
        self.sum = total if self.left() == 0 else total.astype(BF16)

    def wait(self, *others):
        (self.sum,) = together([self.sum], *others)


def meet(rings, *others):
    for ring in rings:
        ring.wait(*(r.before for r in rings if r is not ring), *(others if ring is rings[0] else ()))


def exchanges():
    hops = []
    for axis in ("core", "tensor"):
        distance = 1
        while distance < lax.axis_size(axis):
            hops.append((axis, distance))
            distance *= 2
    return hops


def exchange(values, axis, distance):
    return values + lax.ppermute(values, axis, [(i, i ^ distance) for i in range(lax.axis_size(axis))])


def sum_tensor(values):
    if lax.axis_size("tensor") == 2:
        return values + shift(values, "tensor", 1)
    return lax.psum(values, "tensor")


def body(
    tokens,
    out_grad,
    doc_lengths,
    picture_starts,
    q_weight,
    k_weight,
    v_weight,
    out_weight,
    gate_weight,
    up_weight,
    down_weight,
    attn_in_gain,
    attn_out_gain,
    ffn_in_gain,
    ffn_out_gain,
    query_gain,
    key_gain,
):
    seqs = lax.axis_size("seq")
    cores = lax.axis_size("core")
    tensors = lax.axis_size("tensor")
    s_index = lax.axis_index("seq")
    c_index = lax.axis_index("core")
    t_index = lax.axis_index("tensor")
    micro, per_micro, span, width = tokens.shape
    split_heads = q_weight.shape[1] > HD
    assert q_weight.shape[1] == HD * (cores if split_heads else 1)
    own_feats = k_weight.shape[0]
    feats = own_feats * cores
    hidden_here = gate_weight.shape[1] // cores
    hidden = -(-hidden_here // TILE) * TILE

    def to_columns(arrays, padded):
        parts = [w.reshape(own_feats, cores, -1).transpose(1, 0, 2) for w in arrays]
        parts = [jnp.pad(p, ((0, 0), (0, 0), (0, padded - p.shape[2]))) for p in parts]
        moved = lax.all_to_all(jnp.concatenate(parts, axis=2), "core", split_axis=0, concat_axis=0, tiled=True)
        moved = moved.reshape(feats, -1)
        return [moved[:, i * padded : (i + 1) * padded] for i in range(len(arrays))]

    def to_rows(*arrays):
        values = jnp.concatenate([v.reshape(seqs, span, width) for v in arrays], axis=1)
        moved = lax.all_to_all(values, "seq", split_axis=0, concat_axis=0, tiled=True)
        return [moved[:, i * span : (i + 1) * span].reshape(seqs * span, width) for i in range(len(arrays))]

    def from_rows(values):
        moved = lax.all_to_all(values.reshape(seqs, span, width), "seq", split_axis=0, concat_axis=0, tiled=True)
        return moved.reshape(micro, per_micro, span, width)

    spot_line, spots = ring_spots()
    gains = (attn_in_gain, attn_out_gain, ffn_in_gain, ffn_out_gain, query_gain, key_gain)
    gain_sizes = [v.shape[0] for v in gains]
    gain_ends = [sum(gain_sizes[: i + 1]) for i in range(6)]
    gain_row = sum(jnp.pad(v, (e - n, 2 * HD - e)) for v, e, n in zip(gains, gain_ends, gain_sizes))
    gain_row = jnp.pad(gain_row[None, :], ((0, -(own_feats + 1) % 16), (0, 0)))
    kv_block = jnp.concatenate([jnp.concatenate([k_weight, v_weight], axis=1), gain_row], axis=0)
    some = jnp.concatenate([q_weight, out_weight], axis=1)
    some = jnp.concatenate([kv_block, jnp.pad(some, ((0, kv_block.shape[0] - own_feats), (0, 0)))], axis=1)
    moving = some
    some = put(jnp.zeros((seqs,) + some.shape, BF16), some, 0, spots[0])
    gain_rows = moving[own_feats:, : 2 * HD]
    gain_rows = put(jnp.zeros((seqs,) + gain_rows.shape, BF16), gain_rows, 0, spots[0])
    (x,) = to_rows(tokens)
    for step in range(1, seqs):
        if step == 5:
            moving = together([moving], x)[0]
        moving = hop(moving)
        some = put(some, moving, 0, spots[step])
        gain_rows = put(gain_rows, moving[own_feats:, : 2 * HD], 0, spots[step])
    early = moving
    def with_core(values):
        if cores != 2:
            return lax.all_gather(values, "core", axis=1)
        other = shift(values, "core", 1)
        return jnp.where(c_index == 0, jnp.stack([values, other], axis=1), jnp.stack([other, values], axis=1))

    gain_all = with_core(gain_rows)[:, :, 0].astype(F32)
    some = with_core(some)
    some = some.reshape((seqs * cores,) + some.shape[2:])
    first = 2 * HD + (c_index * HD if split_heads else 0)

    def columns(start, many):
        return lax.dynamic_slice(
            some, (0, 0, start), (seqs * cores, own_feats, many), allow_negative_indices=False
        ).reshape(width, many)

    q_full = columns(first, HD)
    out_full = columns(first + q_weight.shape[1], HD)
    qkv_full = jnp.concatenate([q_full, columns(0, 2 * HD)], axis=1)
    g_in, g_ao, g_fi, g_fo, g_q, g_k = (
        gain_all[:, :, end - size : end].reshape(1, -1) for end, size in zip(gain_ends, gain_sizes)
    )

    size = seqs * span
    group = cores * tensors
    rows = size * group

    owner_tensor = ((t_index - jnp.arange(tensors, dtype=jnp.int32)) % tensors)[:, None, None, None]
    owner_core = ((c_index - jnp.arange(cores, dtype=jnp.int32)) % cores)[None, :, None, None]
    block_index = jnp.arange(seqs, dtype=jnp.int32)[None, None, :, None]
    inner = jnp.arange(span, dtype=jnp.int32)[None, None, None, :]
    places = (((block_index * cores + owner_core) * tensors + owner_tensor) * span + inner).reshape(-1)
    docs, within, pics = layout(
        *(pick(v.reshape(seqs, -1), s_index, 0) for v in (doc_lengths, picture_starts)), places
    )
    frequency = ROPE_BASE ** (-2.0 * jnp.arange(HD // 2, dtype=F32) / HD)
    angles = within.astype(F32)[:, None] * frequency[None, :]
    cosine = jnp.cos(angles)
    sine = jnp.sin(angles)
    meta = [docs, places, pics] + [jnp.zeros_like(docs)] * 5
    meta_q = jnp.stack(meta, axis=1)
    meta_k = jnp.stack(meta, axis=0)
    q_blocks = list(range(group)) if split_heads else [k * cores for k in range(tensors)]
    q_count = len(q_blocks)
    block = struct((size, width), BF16)
    vector = struct((1, width), F32)

    def flat(lists):
        return [p for line in lists for p in line]

    def by_tensor(pieces):
        return [pieces[k * cores : (k + 1) * cores] for k in range(tensors)]

    (a_own,) = small_call(start_kernel, [block], (x, g_in))
    a_all = flat(gather_rows(a_own))
    low_rows = struct((rows, HD), BF16)
    o, prob, raw, query, key, value, *r_parts = small_call(
        functools.partial(attend_kernel, group, q_blocks),
        [struct((q_count * size, HD), BF16), struct((q_count * size, rows), BF16), struct((rows, 2 * HD), BF16)]
        + [low_rows] * 3
        + [block] * q_count,
        (*a_all, qkv_full, out_full, cosine, sine, g_q, g_k, meta_q, meta_k),
        flops=2 * rows * width * 3 * HD + 2 * q_count * size * HD * (2 * rows + width),
    )
    if q_count != group:
        spread = [jnp.zeros((size, width), BF16)] * group
        for i, part in zip(q_blocks, r_parts):
            spread[i] = part
        r_parts = spread
    shares, sent = scatter_rows(by_tensor(r_parts))

    branch, middle, f_own = small_call(
        functools.partial(middle_kernel, len(shares)),
        [struct((size, width), F32)] * 2 + [block],
        (*shares, x, g_ao, g_fi),
    )
    f_all = gather_rows(f_own)

    blocks = to_columns([gate_weight, up_weight, down_weight], hidden)
    moving = together(blocks, early)
    fulls = [put(jnp.zeros((seqs, feats, hidden), BF16), v, 0, spots[0]) for v in moving]
    ahead = {2: (0, [a_own]), 3: (1, [qkv_full, out_full]), 4: (2, sent), 6: (0, [f_own])}
    for step in range(1, seqs):
        if step in ahead:
            chain, values = ahead[step]
            moving = list(moving)
            (moving[chain],) = together([moving[chain]], *values)
        moving = [hop(v) for v in moving]
        if step == seqs - 2:
            nearly = moving
        fulls = [put(full, v, 0, spots[step]) for full, v in zip(fulls, moving)]
    gate_full, up_full, down_full = fulls
    gate_full, up_full, down_full = (w.reshape(width, hidden) for w in (gate_full, up_full, down_full))
    f_pieces = flat(f_all)
    keep_gate, keep_up, hid = hidden_forward(f_pieces, gate_full, up_full)
    (cotangent,) = to_rows(*together([out_grad], *nearly))
    shares, _ = scatter_rows(by_tensor(down_forward(hid, down_full, group)))
    output, de_own, gain_fo = small_call(
        functools.partial(close_kernel, len(shares)),
        [block, block, vector],
        (*shares, middle, cotangent, g_fo),
    )

    output = from_rows(output)
    de_all = flat(gather_rows(de_own))
    downs = RingSum(outer([(de_all, together([hid], output))], spot_line))
    dgate, dup, *df_parts = hidden_backward(
        together(de_all, downs.sum), keep_gate, keep_up, gate_full, up_full, down_full
    )
    downs.step()
    downs.wait(dgate)
    shares, _ = scatter_rows(by_tensor(df_parts))
    gates = RingSum(outer([(f_pieces, together([dgate], downs.sum))], spot_line))
    downs.step()
    downs.wait(gates.sum)
    first_gate = gates.sum
    gates.step()
    ups = RingSum(outer([(f_pieces, together([dup], first_gate, downs.sum))], spot_line))
    downs.step()
    rings = [ups, gates, downs]
    meet(rings)

    def stage():
        for ring in rings:
            if ring.left():
                ring.step()

    stage()
    dmid, dr_own, gain_fi, gain_ao = small_call(
        functools.partial(turn_kernel, len(shares)),
        [struct((size, width), F32), block, vector, vector],
        (*together(shares, ups.blocks[0]), middle, cotangent, branch, g_fi, g_ao),
    )
    meet(rings, dr_own)

    dr_all = flat(gather_rows(dr_own))
    dr_used = [dr_all[i] for i in q_blocks]
    stage()
    grads, gain_q, gain_k, *da_parts = small_call(
        functools.partial(attend_back_kernel, q_count, q_blocks, group),
        [struct((rows, 3 * HD), BF16), struct((1, HD), F32), struct((1, HD), F32)] + [block] * group,
        (
            *dr_used,
            *(prob, raw, query, key, value, qkv_full, out_full, cosine, sine, g_q, g_k),
        ),
        scratch=[pltpu.VMEM((rows, HD), F32)] * 2,
    )
    meet(rings, grads)
    shares, sent = scatter_rows(by_tensor(da_parts))
    stage()
    smalls = RingSum(outer([(a_all, [grads]), (dr_used, [o])], spot_line))
    smalls.step()
    meet(rings, *sent)
    smalls.wait(ups.sum)
    stage()
    smalls.step()
    input_grad, gain_in = small_call(
        functools.partial(last_kernel, len(shares)),
        [block, vector],
        (*shares, x, dmid, g_in),
    )
    gain_grads = (gain_in, gain_ao, gain_fi, gain_fo, gain_q, gain_k)
    packed = jnp.concatenate([g.reshape(seqs * cores, -1) for g in gain_grads], axis=1)
    rings.append(smalls)
    meet(rings, input_grad, packed)
    input_grad = from_rows(input_grad)
    for way in exchanges():
        packed = exchange(packed, *way)
    packed = lax.all_to_all(
        packed.reshape(seqs, cores, -1), "seq", split_axis=0, concat_axis=0, tiled=True
    ).sum(axis=0)
    while ups.left():
        stage()
        meet(rings, *([packed] if ups.left() == 1 else []))
    while smalls.left():
        smalls.step()
    down_sum, small_sum = downs.sum, smalls.sum
    gate_sum, up_sum = gates.sum, ups.sum

    def to_owner(values):
        values = values.astype(F32)
        if cores != 2:
            return lax.all_to_all(values, "core", split_axis=0, concat_axis=1, tiled=True)
        halves = values.reshape(cores, own_feats, -1)
        mine = pick(halves, c_index, 0)
        other = shift(pick(halves, 1 - c_index, 0), "core", 1)
        return jnp.where(
            c_index == 0, jnp.concatenate([mine, other], axis=1), jnp.concatenate([other, mine], axis=1)
        )

    def sum_core(values):
        values = values.astype(F32)
        if cores != 2:
            return lax.psum_scatter(values, "core", scatter_dimension=0, tiled=True)
        halves = values.reshape(cores, own_feats, -1)
        return pick(halves, c_index, 0) + shift(pick(halves, 1 - c_index, 0), "core", 1)

    kv_sum = sum_tensor(sum_core(small_sum[:, HD : 3 * HD]))
    own_columns = to_owner if split_heads else sum_core
    q_grad, out_grad_w = own_columns(small_sum[:, :HD]), own_columns(small_sum[:, 3 * HD :])
    mine = pick(packed, c_index, 0)
    gain_out = tuple(mine[end - n : end] for end, n in zip(gain_ends, gain_sizes))
    return (
        output,
        input_grad,
        q_grad,
        kv_sum[:, :HD],
        kv_sum[:, HD:],
        out_grad_w,
        to_owner(gate_sum[:, :hidden_here]),
        to_owner(up_sum[:, :hidden_here]),
        to_owner(down_sum[:, :hidden_here]),
    ) + gain_out


def solution(mesh):
    def run(tokens, *rest):
        seqs = tokens.shape[0] * tokens.shape[1]
        wide, tensor = mesh.shape["wide"], mesh.shape["tensor"]
        fine = Mesh(mesh.devices.reshape(seqs, wide // seqs, tensor), ("seq", "core", "tensor"))
        acts = P(None, None, ("seq", "core", "tensor"), None)
        both = P(("seq", "core"), "tensor")
        rows = P(("seq", "core"), None)
        vector = P(("seq", "core"))
        weights = (both, rows, rows, both, both, both, both) + (vector,) * 6
        return jax.shard_map(
            body,
            mesh=fine,
            in_specs=(acts, acts, P(), P()) + weights,
            out_specs=(acts, acts) + weights,
            check_vma=False,
        )(tokens, *rest)

    return run
```

```python
import functools

import jax
import jax.numpy as jnp
from jax import lax
from jax.experimental import pallas as pl
from jax.experimental.pallas import tpu as pltpu
from jax.sharding import Mesh
from jax.sharding import PartitionSpec as P

HD = 256
PIC = 256
EPSILON = 1e-06
ROPE_BASE = 1000000.0
SCALE = HD ** (-0.5)
TILE = 256
F32 = jnp.float32
BF16 = jnp.bfloat16


def dot(left, right, dims):
    return lax.dot_general(left, right, ((dims[0], dims[1]), ((), ())), preferred_element_type=F32)


def mm(left, right):
    return dot(left, right, ((1,), (0,)))


def mm_nt(left, right):
    return dot(left, right, ((1,), (1,)))


def mm_tn(left, right):
    return dot(left, right, ((0,), (0,)))


def inverse_root(values):
    return lax.rsqrt(jnp.mean(values * values, axis=-1, keepdims=True) + EPSILON)


def norm_back(values, factor, grad):
    root = inverse_root(values)
    scaled = grad * factor
    inner = jnp.mean(values * scaled, axis=-1, keepdims=True)
    grad_values = root * (scaled - values * (root * root * inner))
    return grad_values, jnp.sum(grad * (values * root), axis=0, keepdims=True)


def turn(values, cosine, sine):
    half = values.shape[-1] // 2
    first = values[..., :half]
    second = values[..., half:]
    return jnp.concatenate([first * cosine - second * sine, second * cosine + first * sine], axis=-1)


def gelu_parts(v):
    c = (2.0 / jnp.pi) ** 0.5
    square = v * v
    t = jnp.tanh(c * v * (1.0 + 0.044715 * square))
    value = 0.5 * v * (1.0 + t)
    slope = 0.5 * (1.0 + t) + 0.5 * v * (1.0 - t * t) * (c * (1.0 + 0.134145 * square))
    return value, slope


def call(kernel, outs, ins, scratch=(), mib=48, flops=0, moved=0, **more):
    return pl.pallas_call(
        kernel,
        out_shape=outs,
        scratch_shapes=list(scratch),
        compiler_params=pltpu.CompilerParams(vmem_limit_bytes=mib << 20),
        cost_estimate=pl.CostEstimate(flops=0, bytes_accessed=1, transcendentals=0),
        **more,
    )(*ins)


def small_call(kernel, outs, ins, **more):
    vmem = pl.BlockSpec(memory_space=pltpu.VMEM)
    moved = sum(v.size * v.dtype.itemsize for v in (*ins, *outs))
    return call(
        kernel, outs, ins, in_specs=[vmem] * len(ins), out_specs=[vmem] * len(outs), moved=moved, **more
    )


def struct(shape, kind):
    return jax.ShapeDtypeStruct(shape, kind)


def total_of(refs):
    total = refs[0][...].astype(F32)
    for ref in refs[1:]:
        total = total + ref[...].astype(F32)
    return total


def start_kernel(x_ref, gain_ref, a_ref):
    x = x_ref[...].astype(F32)
    a_ref[...] = (x * inverse_root(x) * gain_ref[...]).astype(BF16)


def middle_kernel(count, *refs):
    x_ref, g_ao, g_fi = refs[count : count + 3]
    r_ref, mid_ref, f_ref = refs[count + 3 :]
    r = total_of(refs[:count])
    mid = x_ref[...].astype(F32) + r * inverse_root(r) * g_ao[...]
    r_ref[...] = r
    mid_ref[...] = mid
    f_ref[...] = (mid * inverse_root(mid) * g_fi[...]).astype(BF16)


def close_kernel(count, *refs):
    mid_ref, cot_ref, g_fo = refs[count : count + 3]
    out_ref, de_ref, gain_ref = refs[count + 3 :]
    e = total_of(refs[:count])
    cot = cot_ref[...].astype(F32)
    out_ref[...] = (mid_ref[...] + e * inverse_root(e) * g_fo[...]).astype(BF16)
    de, gain = norm_back(e, g_fo[...], cot)
    de_ref[...] = de.astype(BF16)
    gain_ref[...] = gain


def turn_kernel(count, *refs):
    mid_ref, cot_ref, r_ref, g_fi, g_ao = refs[count : count + 5]
    dmid_ref, dr_ref, gain_fi, gain_ao = refs[count + 5 :]
    back, gain = norm_back(mid_ref[...], g_fi[...], total_of(refs[:count]))
    gain_fi[...] = gain
    dmid = cot_ref[...].astype(F32) + back
    dmid_ref[...] = dmid
    dr, gain = norm_back(r_ref[...], g_ao[...], dmid)
    gain_ao[...] = gain
    dr_ref[...] = dr.astype(BF16)


def last_kernel(count, *refs):
    x_ref, dmid_ref, g_in = refs[count : count + 3]
    dx_ref, gain_ref = refs[count + 3 :]
    back, gain = norm_back(x_ref[...].astype(F32), g_in[...], total_of(refs[:count]))
    dx_ref[...] = (dmid_ref[...] + back).astype(BF16)
    gain_ref[...] = gain


def attend_kernel(count, q_blocks, *refs):
    a_refs = refs[:count]
    qkv, out_w, cosine, sine, g_q, g_k, meta_q, meta_k = refs[count : count + 8]
    o_ref, prob_ref, raw_ref, q_ref, k_ref, v_ref = refs[count + 8 : count + 14]
    r_refs = refs[count + 14 :]
    size = a_refs[0].shape[0]
    for i, a_ref in enumerate(a_refs):
        rows = slice(i * size, (i + 1) * size)
        raw = mm(a_ref[...], qkv[...])
        raw_ref[rows] = raw[:, : 2 * HD].astype(BF16)
        cos, sin = cosine[rows], sine[rows]
        query, key = raw[:, :HD], raw[:, HD : 2 * HD]
        q_ref[rows] = (turn(query * inverse_root(query) * g_q[...], cos, sin) * SCALE).astype(BF16)
        k_ref[rows] = turn(key * inverse_root(key) * g_k[...], cos, sin).astype(BF16)
        v_ref[rows] = raw[:, 2 * HD :].astype(BF16)
    key_doc, key_place, key_pic = meta_k[0:1], meta_k[1:2], meta_k[2:3]
    for n, i in enumerate(q_blocks):
        rows = slice(i * size, (i + 1) * size)
        done = slice(n * size, (n + 1) * size)
        scores = mm_nt(q_ref[rows], k_ref[...])
        doc, place, pic = meta_q[rows, 0:1], meta_q[rows, 1:2], meta_q[rows, 2:3]
        allowed = (doc == key_doc) & ((key_place <= place) | ((pic == key_pic) & (pic >= 0)))
        scores = jnp.where(allowed, scores, -1e30)
        weight = jnp.exp(scores - jnp.max(scores, axis=-1, keepdims=True))
        prob = (weight * (1.0 / jnp.sum(weight, axis=-1, keepdims=True))).astype(BF16)
        prob_ref[done] = prob
        o = mm(prob, v_ref[...]).astype(BF16)
        o_ref[done] = o
        r_refs[n][...] = mm_nt(o, out_w[...]).astype(BF16)


def attend_back_kernel(count, q_blocks, total, *refs):
    dr_refs = refs[:count]
    prob_ref, raw_ref, q_ref, k_ref, v_ref, qkv, out_w, cosine, sine, g_q, g_k = refs[count : count + 11]
    grad_ref, gain_q, gain_k = refs[count + 11 : count + 14]
    da_refs = refs[count + 14 : count + 14 + total]
    dk_ref, dv_ref = refs[count + 14 + total :]
    size = dr_refs[0].shape[0]
    if len(q_blocks) != total:
        grad_ref[:, :HD] = jnp.zeros((size * total, HD), BF16)
    sum_q = jnp.zeros((1, HD), F32)
    sum_k = jnp.zeros((1, HD), F32)
    for n, i in enumerate(q_blocks):
        rows = slice(i * size, (i + 1) * size)
        done = slice(n * size, (n + 1) * size)
        do = mm(dr_refs[n][...], out_w[...]).astype(BF16)
        prob_low = prob_ref[done]
        prob = prob_low.astype(F32)
        dprob = mm_nt(do, v_ref[...])
        ds = (prob * (dprob - jnp.sum(prob * dprob, axis=-1, keepdims=True))).astype(BF16)
        dq = mm(ds, k_ref[...])
        dk = mm_tn(ds, q_ref[rows])
        dv = mm_tn(prob_low, do)
        if n == 0:
            dk_ref[...] = dk
            dv_ref[...] = dv
        else:
            dk_ref[...] += dk
            dv_ref[...] += dv
        raw = raw_ref[rows, :HD].astype(F32)
        back, gain = norm_back(raw, g_q[...], turn(dq * SCALE, cosine[rows], -sine[rows]))
        grad_ref[rows, :HD] = back.astype(BF16)
        sum_q = sum_q + gain
    for i in range(total):
        rows = slice(i * size, (i + 1) * size)
        raw = raw_ref[rows, HD:].astype(F32)
        back, gain = norm_back(raw, g_k[...], turn(dk_ref[rows], cosine[rows], -sine[rows]))
        grad_ref[rows, HD : 2 * HD] = back.astype(BF16)
        grad_ref[rows, 2 * HD :] = dv_ref[rows].astype(BF16)
        sum_k = sum_k + gain
        da_refs[i][...] = mm_nt(grad_ref[rows], qkv[...]).astype(BF16)
    gain_q[...] = sum_q
    gain_k[...] = sum_k


def hidden_kernel(count, *refs):
    gate_w, up_w, keep_gate, keep_up, hid_ref = refs[count:]
    size = refs[0].shape[0]
    for i in range(count):
        rows = slice(i * size, (i + 1) * size)
        gate = mm(refs[i][...], gate_w[...])
        up = mm(refs[i][...], up_w[...])
        value, slope = gelu_parts(gate)
        keep_gate[rows] = (up * slope).astype(BF16)
        keep_up[rows] = value.astype(BF16)
        hid_ref[rows] = (value * up).astype(BF16)


def down_kernel(hid_ref, down_w, *outs):
    size = outs[0].shape[0]
    part = mm_nt(hid_ref[...], down_w[...]).astype(BF16)
    for i, out in enumerate(outs):
        out[...] = part[i * size : (i + 1) * size]


def hidden_back_kernel(count, *refs):
    keep_gate, keep_up, gate_w, up_w, down_w, dgate_ref, dup_ref = refs[count : count + 7]
    df_refs = refs[count + 7 :]
    size = refs[0].shape[0]
    for i in range(count):
        rows = slice(i * size, (i + 1) * size)
        dhid = mm(refs[i][...], down_w[...])
        dgate_ref[rows] = (dhid * keep_gate[rows].astype(F32)).astype(BF16)
        dup_ref[rows] = (dhid * keep_up[rows].astype(F32)).astype(BF16)
        df_refs[i][...] = (mm_nt(dgate_ref[rows], gate_w[...]) + mm_nt(dup_ref[rows], up_w[...])).astype(BF16)


def hidden_forward(pieces, gate_w, up_w):
    size, hidden = pieces[0].shape[0], gate_w.shape[1]
    return small_call(
        functools.partial(hidden_kernel, len(pieces)),
        [struct((len(pieces) * size, hidden), BF16)] * 3,
        (*pieces, gate_w, up_w),
        mib=24,
    )


def down_forward(hid, down_w, count):
    shape = hid.shape[0] // count, down_w.shape[0]
    return small_call(down_kernel, [struct(shape, BF16)] * count, (hid, down_w), mib=24)


def hidden_backward(pieces, keep_gate, keep_up, gate_w, up_w, down_w):
    size, width = pieces[0].shape
    count, hidden = len(pieces), gate_w.shape[1]
    return small_call(
        functools.partial(hidden_back_kernel, count),
        [struct((count * size, hidden), BF16)] * 2 + [struct((size, width), BF16)] * count,
        (*pieces, keep_gate, keep_up, gate_w, up_w, down_w),
        mib=24,
    )


def outer_kernel(groups, spots, *refs):
    count = spots.shape[0]
    outs, whole, sems = refs[-2 - count : -2], refs[-2], refs[-1]
    feats = whole.shape[0] // count
    used, column, copies = 0, 0, []
    for n, (lefts, rights) in enumerate(groups):
        left = jnp.concatenate([r[...] for r in refs[used : used + lefts]], axis=0)
        right = jnp.concatenate([r[...] for r in refs[used + lefts : used + lefts + rights]], axis=0)
        columns = slice(column, column + right.shape[1])
        whole[:, columns] = mm_tn(left, right).astype(BF16)
        for k, out in enumerate(outs):
            first = pl.multiple_of(spots[(k + 1) % count] * feats, 16)
            copies.append(
                pltpu.make_async_copy(whole.at[pl.ds(first, feats), columns], out.at[:, columns], sems.at[n, k])
            )
            copies[-1].start()
        used, column = used + lefts + rights, columns.stop
    for copy in copies:
        copy.wait()


def outer(products, spots):
    count = spots.shape[0]
    width = products[0][0][0].shape[1]
    total = sum(right[0].shape[1] for _, right in products)
    ins = [v for left, right in products for v in (*left, *right)]
    vmem = pl.BlockSpec(memory_space=pltpu.VMEM)
    return call(
        functools.partial(outer_kernel, [(len(left), len(right)) for left, right in products]),
        [struct((width // count, total), BF16)] * count,
        (spots, *ins),
        scratch=[pltpu.VMEM((width, total), BF16), pltpu.SemaphoreType.DMA((len(products), count))],
        in_specs=[pl.BlockSpec(memory_space=pltpu.SMEM)] + [vmem] * len(ins),
        out_specs=[pl.BlockSpec(memory_space=pl.ANY)] * count,
        mib=32,
    )


def layout(lengths, starts, places):
    doc_ends = jnp.cumsum(lengths)
    before = places[:, None] >= doc_ends[None, :]
    doc_ids = jnp.sum(before.astype(jnp.int32), axis=1)
    opening = jnp.max(jnp.where(before, doc_ends[None, :], 0), axis=1)
    inside = (places[:, None] >= starts[None, :]) & (places[:, None] < starts[None, :] + PIC)
    labels = jnp.arange(1, starts.shape[0] + 1, dtype=jnp.int32)
    pictures = jnp.sum(jnp.where(inside, labels[None, :], 0), axis=1) - 1
    return doc_ids, places - opening, pictures


def shift(values, axis, step):
    size = lax.axis_size(axis)
    return lax.ppermute(values, axis, [(i, (i + step) % size) for i in range(size)])


def gather_rows(own):
    across = [own] + [shift(own, "tensor", k) for k in range(1, lax.axis_size("tensor"))]
    return [[p] + [shift(p, "core", k) for k in range(1, lax.axis_size("core"))] for p in across]


def scatter_rows(parts):
    result, sent = [], []
    for k in list(range(1, len(parts))) + [0]:
        first = [parts[k][0]] + [shift(p, "core", -j) for j, p in enumerate(parts[k]) if j]
        if k:
            total = first[0].astype(F32)
            for p in first[1:]:
                total = total + p.astype(F32)
            sent.append(total.astype(BF16))
            result.append(shift(sent[-1], "tensor", -k))
        else:
            result.extend(first)
    return result, sent


def ring_order(count):
    return list(range(0, count, 2)) + list(range(1, count, 2))[::-1]


def ring_spots():
    count = lax.axis_size("seq")
    ring = ring_order(count)
    table = [
        [[ring[(ring.index(i) - way * k) % count] for k in range(count)] for i in range(count)] for way in (1, -1)
    ]
    line = jnp.array(table, jnp.int32).reshape(2 * count, count)
    row = (lax.axis_index("core") % 2) * count + lax.axis_index("seq")
    line = lax.dynamic_index_in_dim(line, row, 0, keepdims=False, allow_negative_indices=False)
    return line, [line[k] for k in range(count)]


def together(values, *others):
    return lax.optimization_barrier((tuple(values), others))[0]


def hop(values):
    count, cores = lax.axis_size("seq"), lax.axis_size("core")
    ring = ring_order(count)
    pairs = [
        (ring[i] * cores + c, ring[(i + (-1) ** (c % 2)) % count] * cores + c)
        for i in range(count)
        for c in range(cores)
    ]
    return lax.ppermute(values, ("seq", "core"), pairs)


def put(full, block, row, spot):
    return lax.dynamic_update_slice(full, block[None], (spot, row, 0), allow_negative_indices=False)


def pick(array, spot, axis):
    return lax.dynamic_index_in_dim(array, spot, axis, keepdims=False, allow_negative_indices=False)


class RingSum:
    def __init__(self, blocks):
        self.blocks, self.hops = blocks, 0
        self.sum = self.before = blocks[0]

    def left(self):
        return len(self.blocks) - 1 - self.hops

    def step(self):
        self.hops += 1
        self.before = self.sum
        total = hop(self.sum).astype(F32) + self.blocks[self.hops].astype(F32)
        self.sum = total if self.left() == 0 else total.astype(BF16)

    def wait(self, *others):
        (self.sum,) = together([self.sum], *others)


def meet(rings, *others):
    for ring in rings:
        ring.wait(*(r.before for r in rings if r is not ring), *(others if ring is rings[0] else ()))


def exchanges():
    hops = []
    for axis in ("core", "tensor"):
        distance = 1
        while distance < lax.axis_size(axis):
            hops.append((axis, distance))
            distance *= 2
    return hops


def exchange(values, axis, distance):
    return values + lax.ppermute(values, axis, [(i, i ^ distance) for i in range(lax.axis_size(axis))])


def sum_tensor(values):
    if lax.axis_size("tensor") == 2:
        return values + shift(values, "tensor", 1)
    return lax.psum(values, "tensor")


def body(
    tokens,
    out_grad,
    doc_lengths,
    picture_starts,
    q_weight,
    k_weight,
    v_weight,
    out_weight,
    gate_weight,
    up_weight,
    down_weight,
    attn_in_gain,
    attn_out_gain,
    ffn_in_gain,
    ffn_out_gain,
    query_gain,
    key_gain,
):
    seqs = lax.axis_size("seq")
    cores = lax.axis_size("core")
    tensors = lax.axis_size("tensor")
    s_index = lax.axis_index("seq")
    c_index = lax.axis_index("core")
    t_index = lax.axis_index("tensor")
    micro, per_micro, span, width = tokens.shape
    split_heads = q_weight.shape[1] > HD
    assert q_weight.shape[1] == HD * (cores if split_heads else 1)
    own_feats = k_weight.shape[0]
    feats = own_feats * cores
    hidden_here = gate_weight.shape[1] // cores
    hidden = -(-hidden_here // TILE) * TILE

    def to_columns(arrays, padded):
        parts = [w.reshape(own_feats, cores, -1).transpose(1, 0, 2) for w in arrays]
        parts = [jnp.pad(p, ((0, 0), (0, 0), (0, padded - p.shape[2]))) for p in parts]
        moved = lax.all_to_all(jnp.concatenate(parts, axis=2), "core", split_axis=0, concat_axis=0, tiled=True)
        moved = moved.reshape(feats, -1)
        return [moved[:, i * padded : (i + 1) * padded] for i in range(len(arrays))]

    def to_rows(*arrays):
        values = jnp.concatenate([v.reshape(seqs, span, width) for v in arrays], axis=1)
        moved = lax.all_to_all(values, "seq", split_axis=0, concat_axis=0, tiled=True)
        return [moved[:, i * span : (i + 1) * span].reshape(seqs * span, width) for i in range(len(arrays))]

    def from_rows(values):
        moved = lax.all_to_all(values.reshape(seqs, span, width), "seq", split_axis=0, concat_axis=0, tiled=True)
        return moved.reshape(micro, per_micro, span, width)

    spot_line, spots = ring_spots()
    gains = (attn_in_gain, attn_out_gain, ffn_in_gain, ffn_out_gain, query_gain, key_gain)
    gain_sizes = [v.shape[0] for v in gains]
    gain_ends = [sum(gain_sizes[: i + 1]) for i in range(6)]
    gain_row = sum(jnp.pad(v, (e - n, 2 * HD - e)) for v, e, n in zip(gains, gain_ends, gain_sizes))
    gain_row = jnp.pad(gain_row[None, :], ((0, -(own_feats + 1) % 16), (0, 0)))
    kv_block = jnp.concatenate([jnp.concatenate([k_weight, v_weight], axis=1), gain_row], axis=0)
    some = jnp.concatenate([q_weight, out_weight], axis=1)
    some = jnp.concatenate([kv_block, jnp.pad(some, ((0, kv_block.shape[0] - own_feats), (0, 0)))], axis=1)
    moving = some
    some = put(jnp.zeros((seqs,) + some.shape, BF16), some, 0, spots[0])
    gain_rows = moving[own_feats:, : 2 * HD]
    gain_rows = put(jnp.zeros((seqs,) + gain_rows.shape, BF16), gain_rows, 0, spots[0])
    (x,) = to_rows(tokens)
    for step in range(1, seqs):
        if step == 5:
            moving = together([moving], x)[0]
        moving = hop(moving)
        some = put(some, moving, 0, spots[step])
        gain_rows = put(gain_rows, moving[own_feats:, : 2 * HD], 0, spots[step])
    early = moving
    def with_core(values):
        if cores != 2:
            return lax.all_gather(values, "core", axis=1)
        other = shift(values, "core", 1)
        return jnp.where(c_index == 0, jnp.stack([values, other], axis=1), jnp.stack([other, values], axis=1))

    gain_all = with_core(gain_rows)[:, :, 0].astype(F32)
    some = with_core(some)
    some = some.reshape((seqs * cores,) + some.shape[2:])
    first = 2 * HD + (c_index * HD if split_heads else 0)

    def columns(start, many):
        return lax.dynamic_slice(
            some, (0, 0, start), (seqs * cores, own_feats, many), allow_negative_indices=False
        ).reshape(width, many)

    q_full = columns(first, HD)
    out_full = columns(first + q_weight.shape[1], HD)
    qkv_full = jnp.concatenate([q_full, columns(0, 2 * HD)], axis=1)
    g_in, g_ao, g_fi, g_fo, g_q, g_k = (
        gain_all[:, :, end - size : end].reshape(1, -1) for end, size in zip(gain_ends, gain_sizes)
    )

    size = seqs * span
    group = cores * tensors
    rows = size * group

    owner_tensor = ((t_index - jnp.arange(tensors, dtype=jnp.int32)) % tensors)[:, None, None, None]
    owner_core = ((c_index - jnp.arange(cores, dtype=jnp.int32)) % cores)[None, :, None, None]
    block_index = jnp.arange(seqs, dtype=jnp.int32)[None, None, :, None]
    inner = jnp.arange(span, dtype=jnp.int32)[None, None, None, :]
    places = (((block_index * cores + owner_core) * tensors + owner_tensor) * span + inner).reshape(-1)
    docs, within, pics = layout(
        *(pick(v.reshape(seqs, -1), s_index, 0) for v in (doc_lengths, picture_starts)), places
    )
    frequency = ROPE_BASE ** (-2.0 * jnp.arange(HD // 2, dtype=F32) / HD)
    angles = within.astype(F32)[:, None] * frequency[None, :]
    cosine = jnp.cos(angles)
    sine = jnp.sin(angles)
    meta = [docs, places, pics] + [jnp.zeros_like(docs)] * 5
    meta_q = jnp.stack(meta, axis=1)
    meta_k = jnp.stack(meta, axis=0)
    q_blocks = list(range(group)) if split_heads else [k * cores for k in range(tensors)]
    q_count = len(q_blocks)
    block = struct((size, width), BF16)
    vector = struct((1, width), F32)

    def flat(lists):
        return [p for line in lists for p in line]

    def by_tensor(pieces):
        return [pieces[k * cores : (k + 1) * cores] for k in range(tensors)]

    (a_own,) = small_call(start_kernel, [block], (x, g_in))
    a_all = flat(gather_rows(a_own))
    low_rows = struct((rows, HD), BF16)
    o, prob, raw, query, key, value, *r_parts = small_call(
        functools.partial(attend_kernel, group, q_blocks),
        [struct((q_count * size, HD), BF16), struct((q_count * size, rows), BF16), struct((rows, 2 * HD), BF16)]
        + [low_rows] * 3
        + [block] * q_count,
        (*a_all, qkv_full, out_full, cosine, sine, g_q, g_k, meta_q, meta_k),
        flops=2 * rows * width * 3 * HD + 2 * q_count * size * HD * (2 * rows + width),
    )
    if q_count != group:
        spread = [jnp.zeros((size, width), BF16)] * group
        for i, part in zip(q_blocks, r_parts):
            spread[i] = part
        r_parts = spread
    shares, sent = scatter_rows(by_tensor(r_parts))

    branch, middle, f_own = small_call(
        functools.partial(middle_kernel, len(shares)),
        [struct((size, width), F32)] * 2 + [block],
        (*shares, x, g_ao, g_fi),
    )
    f_all = gather_rows(f_own)

    blocks = to_columns([gate_weight, up_weight, down_weight], hidden)
    moving = together(blocks, early)
    fulls = [put(jnp.zeros((seqs, feats, hidden), BF16), v, 0, spots[0]) for v in moving]
    ahead = {2: (0, [a_own]), 3: (1, [qkv_full, out_full]), 4: (2, sent), 6: (0, [f_own])}
    for step in range(1, seqs):
        if step in ahead:
            chain, values = ahead[step]
            moving = list(moving)
            (moving[chain],) = together([moving[chain]], *values)
        moving = [hop(v) for v in moving]
        if step == seqs - 2:
            nearly = moving
        fulls = [put(full, v, 0, spots[step]) for full, v in zip(fulls, moving)]
    gate_full, up_full, down_full = fulls
    gate_full, up_full, down_full = (w.reshape(width, hidden) for w in (gate_full, up_full, down_full))
    f_pieces = flat(f_all)
    keep_gate, keep_up, hid = hidden_forward(f_pieces, gate_full, up_full)
    (cotangent,) = to_rows(*together([out_grad], *nearly))
    shares, _ = scatter_rows(by_tensor(down_forward(hid, down_full, group)))
    output, de_own, gain_fo = small_call(
        functools.partial(close_kernel, len(shares)),
        [block, block, vector],
        (*shares, middle, cotangent, g_fo),
    )

    output = from_rows(output)
    de_all = flat(gather_rows(de_own))
    downs = RingSum(outer([(de_all, together([hid], output))], spot_line))
    dgate, dup, *df_parts = hidden_backward(
        together(de_all, downs.sum), keep_gate, keep_up, gate_full, up_full, down_full
    )
    downs.step()
    downs.wait(dgate)
    shares, _ = scatter_rows(by_tensor(df_parts))
    gates = RingSum(outer([(f_pieces, together([dgate], downs.sum))], spot_line))
    downs.step()
    downs.wait(gates.sum)
    first_gate = gates.sum
    gates.step()
    ups = RingSum(outer([(f_pieces, together([dup], first_gate, downs.sum))], spot_line))
    downs.step()
    rings = [ups, gates, downs]
    meet(rings)

    def stage():
        for ring in rings:
            if ring.left():
                ring.step()

    stage()
    dmid, dr_own, gain_fi, gain_ao = small_call(
        functools.partial(turn_kernel, len(shares)),
        [struct((size, width), F32), block, vector, vector],
        (*together(shares, ups.blocks[0]), middle, cotangent, branch, g_fi, g_ao),
    )
    meet([downs, ups, gates], dr_own)

    dr_all = flat(gather_rows(dr_own))
    dr_used = [dr_all[i] for i in q_blocks]
    stage()
    grads, gain_q, gain_k, *da_parts = small_call(
        functools.partial(attend_back_kernel, q_count, q_blocks, group),
        [struct((rows, 3 * HD), BF16), struct((1, HD), F32), struct((1, HD), F32)] + [block] * group,
        (
            *dr_used,
            *(prob, raw, query, key, value, qkv_full, out_full, cosine, sine, g_q, g_k),
        ),
        scratch=[pltpu.VMEM((rows, HD), F32)] * 2,
    )
    meet([downs, ups, gates], grads)
    shares, sent = scatter_rows(by_tensor(da_parts))
    stage()
    smalls = RingSum(outer([(a_all, [grads]), (dr_used, [o])], spot_line))
    smalls.step()
    meet([downs, ups, gates], *sent)
    smalls.wait(ups.sum)
    stage()
    smalls.step()
    input_grad, gain_in = small_call(
        functools.partial(last_kernel, len(shares)),
        [block, vector],
        (*shares, x, dmid, g_in),
    )
    gain_grads = (gain_in, gain_ao, gain_fi, gain_fo, gain_q, gain_k)
    packed = jnp.concatenate([g.reshape(seqs * cores, -1) for g in gain_grads], axis=1)
    rings.append(smalls)
    meet(rings, input_grad, packed)
    input_grad = from_rows(input_grad)
    for way in exchanges():
        packed = exchange(packed, *way)
    packed = lax.all_to_all(
        packed.reshape(seqs, cores, -1), "seq", split_axis=0, concat_axis=0, tiled=True
    ).sum(axis=0)
    while ups.left():
        stage()
        meet(rings, *([packed] if ups.left() == 1 else []))
    while smalls.left():
        smalls.step()
    down_sum, small_sum = downs.sum, smalls.sum
    gate_sum, up_sum = gates.sum, ups.sum

    def to_owner(values):
        values = values.astype(F32)
        if cores != 2:
            return lax.all_to_all(values, "core", split_axis=0, concat_axis=1, tiled=True)
        halves = values.reshape(cores, own_feats, -1)
        mine = pick(halves, c_index, 0)
        other = shift(pick(halves, 1 - c_index, 0), "core", 1)
        return jnp.where(
            c_index == 0, jnp.concatenate([mine, other], axis=1), jnp.concatenate([other, mine], axis=1)
        )

    def sum_core(values):
        values = values.astype(F32)
        if cores != 2:
            return lax.psum_scatter(values, "core", scatter_dimension=0, tiled=True)
        halves = values.reshape(cores, own_feats, -1)
        return pick(halves, c_index, 0) + shift(pick(halves, 1 - c_index, 0), "core", 1)

    kv_sum = sum_tensor(sum_core(small_sum[:, HD : 3 * HD]))
    own_columns = to_owner if split_heads else sum_core
    q_grad, out_grad_w = own_columns(small_sum[:, :HD]), own_columns(small_sum[:, 3 * HD :])
    mine = pick(packed, c_index, 0)
    gain_out = tuple(mine[end - n : end] for end, n in zip(gain_ends, gain_sizes))
    return (
        output,
        input_grad,
        q_grad,
        kv_sum[:, :HD],
        kv_sum[:, HD:],
        out_grad_w,
        to_owner(gate_sum[:, :hidden_here]),
        to_owner(up_sum[:, :hidden_here]),
        to_owner(down_sum[:, :hidden_here]),
    ) + gain_out


def solution(mesh):
    def run(tokens, *rest):
        seqs = tokens.shape[0] * tokens.shape[1]
        wide, tensor = mesh.shape["wide"], mesh.shape["tensor"]
        fine = Mesh(mesh.devices.reshape(seqs, wide // seqs, tensor), ("seq", "core", "tensor"))
        acts = P(None, None, ("seq", "core", "tensor"), None)
        both = P(("seq", "core"), "tensor")
        rows = P(("seq", "core"), None)
        vector = P(("seq", "core"))
        weights = (both, rows, rows, both, both, both, both) + (vector,) * 6
        return jax.shard_map(
            body,
            mesh=fine,
            in_specs=(acts, acts, P(), P()) + weights,
            out_specs=(acts, acts) + weights,
            check_vma=False,
        )(tokens, *rest)

    return run
```
